32 devices in a mesh: space: 8 (over z, x), mode: 4 (over y, core).
Axes of the slice: x: 2, y: 2, z: 4, core: 2. Of those that a mesh axis runs over, the one named last changes fastest.
Arguments:
- modes_in: bfloat16 [120, 16384], P('mode', 'space'), may hold values from -6 to 6
- blocks: bfloat16 [5, 576, 128, 128], P(None, 'space'), may hold values from -0.25 to 0.25
- block_cols: int32 [144, 4], P('space'), may hold values from 0 to 15
- send_slot: int32 [2048], P('space'), may hold values from 0 to 511, as said below
- recv_row: int32 [4096], P('space'), may hold values from 0 to 2048, as said below
- mix_cols: int32 [5, 120, 8], replicated, may hold values from 0 to 120, as said below
- mix_coef: float32 [5, 120, 8], replicated, as said below
Outputs:
- first_apply: bfloat16 [120, 16384], P('mode', 'space')
- second_apply: bfloat16 [120, 16384], P('mode', 'space')
The draws below stay inside these ranges and needn't reach their ends.
Inputs may be any that keep to these rules, and one draw needn't show every extreme that they name: Interface row e of subdomain d goes to subdomain send_slot[d * 256 + e] // 64 at position send_slot[d * 256 + e] % 64. A subdomain's entries are distinct, and for each destination they fill positions from 0 upward, at most 64; one destination, the same for all subdomains, gets 64 rows from every subdomain. `recv_row`: entry o * 8 * 64 + d * 64 + p is the own degree of freedom of subdomain o at which position p from subdomain d is added; it is 2048 exactly where subdomain d sends fewer than p + 1 rows to o. Live entries may repeat. `mix_cols`: column 120 marks a padded slot. Each row of each term has from 4 to 8 live slots, both reached; live columns may repeat. `mix_coef`: zero exactly on padded slots.
All inputs are finite; a program needn't handle non-finite values.
Results may differ from the reference program's by a relative error of at most 0.022.
Values may be sent and summed in bfloat16 or wider, within the bound.
A program may use at most 64 MiB of HBM per device.

```python
import jax
import jax.numpy as jnp
from jax import lax

P_SIZE = 120
TERMS = 5
BLK = 128
NZ_ROW = 4
NNZ_C = 8
B_DEV = 16
OUT_BLOCKS = 18
D_OWN = 2048
IF_DEV = 256
CAP = 64
N_DOF = 16384
N_SPACE = 8


def pair_counts(key):
    count_key = jax.random.fold_in(key, 11)
    half_cap = CAP // 2
    offsets = jax.random.randint(jax.random.fold_in(count_key, 1), (N_SPACE, N_SPACE // 2), -half_cap, half_cap + 1)
    chosen = jax.random.randint(jax.random.fold_in(count_key, 2), (), 0, N_SPACE // 2)
    side_bit = jax.random.randint(jax.random.fold_in(count_key, 3), (), 0, 2)
    pair_ids = jnp.arange(N_SPACE // 2)
    forced = half_cap - 2 * half_cap * side_bit
    offsets = jnp.where(pair_ids[None, :] == chosen, forced, offsets)
    return jnp.stack([half_cap + offsets, half_cap - offsets], axis=-1).reshape(N_SPACE, N_SPACE)


def draw_send_slot(key, part):
    counts = pair_counts(key)
    slot_ids = jnp.arange(N_SPACE * CAP)
    position = slot_ids % CAP
    target_dev = slot_ids // CAP
    valid_slot = position[None, :] < counts[:, target_dev]
    order_keys = jnp.where(valid_slot, slot_ids[None, :], slot_ids[None, :] + N_SPACE * CAP)
    ordered = jnp.sort(order_keys, axis=1)[:, :IF_DEV]
    perm_keys = jax.random.split(jax.random.fold_in(key, 12), N_SPACE)
    shuffled = jax.vmap(lambda one_key, slot_row: jax.random.permutation(one_key, slot_row))(perm_keys, ordered)
    return shuffled.reshape(-1).astype(jnp.int32)


def draw_recv_row(key, part):
    counts = pair_counts(key)
    targets = jax.random.randint(jax.random.fold_in(key, 13), (N_SPACE, N_SPACE, CAP), 0, D_OWN)
    live_slot = jnp.arange(CAP)[None, None, :] < counts.T[:, :, None]
    return jnp.where(live_slot, targets, D_OWN).reshape(-1).astype(jnp.int32)


def chaos_live(key):
    live_key = jax.random.fold_in(key, 21)
    live_counts = jax.random.randint(live_key, (TERMS, P_SIZE), NNZ_C // 2, NNZ_C + 1)
    row_ids = jnp.arange(P_SIZE)
    live_counts = jnp.where(row_ids[None, :] % 3 == 0, NNZ_C, live_counts)
    live_counts = jnp.where(row_ids[None, :] % 3 == 1, NNZ_C // 2, live_counts)
    return jnp.arange(NNZ_C)[None, None, :] < live_counts[:, :, None]


def draw_mix_cols(key, part):
    live_slot = chaos_live(key)
    picks = jax.random.randint(jax.random.fold_in(key, 22), (TERMS, P_SIZE, NNZ_C), 0, P_SIZE)
    picks = picks.at[0, :, 0].set(jnp.arange(P_SIZE))
    return jnp.where(live_slot, picks, P_SIZE).astype(jnp.int32)


def draw_mix_coef(key, part):
    live_slot = chaos_live(key)
    sign_key = jax.random.fold_in(key, 23)
    size_key = jax.random.fold_in(key, 24)
    signs = jnp.where(jax.random.bernoulli(sign_key, 0.5, (TERMS, P_SIZE, NNZ_C)), 1.0, -1.0)
    magnitude = jax.random.uniform(size_key, (TERMS, P_SIZE, NNZ_C), jnp.float32, 0.5, 1.5)
    scaled = signs * magnitude / jnp.sqrt(0.75 * TERMS * NNZ_C)
    return jnp.where(live_slot, scaled, 0.0).astype(jnp.float32)


def place_ends(result, stream_key, least, largest):
    index_at = [jax.random.randint(jax.random.fold_in(stream_key, axis), (), 0, length) for axis, length in enumerate(result.shape)]
    widest = result.shape.index(max(result.shape))
    beside = index_at[:widest] + [(index_at[widest] + 1) % result.shape[widest]] + index_at[widest + 1:]
    return result.at[tuple(index_at)].set(least).at[tuple(beside)].set(largest)


def level_of(stream_key, shape, pieces, smallest, top_value):
    loudness = 1.0
    for axis_at, shards_of in pieces:
        steps = jax.random.uniform(jax.random.fold_in(jax.random.fold_in(stream_key, 6), axis_at), (shards_of,), jnp.float32, smallest / len(pieces), top_value / len(pieces))
        loudness = loudness * jnp.repeat(jnp.exp(steps), shape[axis_at] // shards_of).reshape((-1,) + (1,) * (len(shape) - 1 - axis_at))
    return loudness


def centred(own_key, shape, width, most, shards=(), kind=jnp.bfloat16):
    values = width * jax.random.normal(own_key, shape, jnp.float32)
    if shards:
        values = values * level_of(own_key, shape, shards, -0.22, 0.18)
    return jnp.clip(values, -most, most).astype(kind)


def setup_inputs(seed: int = 0) -> dict:
    key_list = jax.random.split(jax.random.key(seed), 8)
    modes_in = centred(key_list[0], (P_SIZE, N_DOF), 1.0, 6.0, ((0, 4), (1, 8)))
    blocks = centred(key_list[1], (TERMS, N_SPACE * OUT_BLOCKS * NZ_ROW, BLK, BLK), (NZ_ROW * BLK) ** -0.5, 0.25, ((1, 8),))
    block_cols = place_ends(jax.random.randint(key_list[2], (N_SPACE * OUT_BLOCKS, NZ_ROW), 0, B_DEV), jax.random.fold_in(key_list[2], 1), 0, B_DEV - 1).astype(jnp.int32)
    send_slot = draw_send_slot(jax.random.fold_in(key_list[7], 71), 0)
    recv_row = draw_recv_row(jax.random.fold_in(key_list[7], 71), 0)
    mix_cols = draw_mix_cols(jax.random.fold_in(key_list[7], 71), 0)
    mix_coef = draw_mix_coef(jax.random.fold_in(key_list[7], 71), 0)
    return {"modes_in": modes_in, "blocks": blocks, "block_cols": block_cols, "send_slot": send_slot, "recv_row": recv_row, "mix_cols": mix_cols, "mix_coef": mix_coef}


def dense_mixer(mix_cols, mix_coef):
    columns = jnp.arange(P_SIZE, dtype=jnp.int32)
    onehot_table = (mix_cols[..., None] == columns).astype(jnp.float32)
    return jnp.sum(mix_coef[..., None] * onehot_table, axis=2).astype(jnp.bfloat16)


def device_products(operands):
    field_dev, stiff_dev, cols_dev = operands
    picked = field_dev[:, :, cols_dev, :].astype(jnp.float32)
    return jnp.einsum('kmcnd,kcnde->mce', picked, stiff_dev.astype(jnp.float32))


def reference(modes_in, blocks, block_cols, send_slot, recv_row, mix_cols, mix_coef):
    chaos_mixer = dense_mixer(mix_cols, mix_coef)
    stiffness = blocks.reshape(TERMS, N_SPACE, OUT_BLOCKS, NZ_ROW, BLK, BLK).transpose(1, 0, 2, 3, 4, 5)
    col_lists = block_cols.reshape(N_SPACE, OUT_BLOCKS, NZ_ROW)
    slot_lists = send_slot.reshape(N_SPACE, IF_DEV)
    recv_lists = recv_row.reshape(N_SPACE, N_SPACE * CAP)
    dest_dev = (slot_lists // CAP).astype(jnp.int32)
    slot_pos = (slot_lists % CAP).astype(jnp.int32)
    source_dev = jnp.arange(N_SPACE, dtype=jnp.int32)[:, None]
    target_row = recv_lists[dest_dev, source_dev * CAP + slot_pos]
    global_row = jnp.where(target_row < D_OWN, dest_dev * D_OWN + target_row, N_DOF).reshape(-1).astype(jnp.int32)

    def one_apply(field_now):
        mixed_field = jnp.einsum('kij,jn->kin', chaos_mixer.astype(jnp.float32), field_now.astype(jnp.float32)).astype(jnp.bfloat16)
        per_device = mixed_field.reshape(TERMS, P_SIZE, N_SPACE, B_DEV, BLK).transpose(2, 0, 1, 3, 4)
        products = lax.map(device_products, (per_device, stiffness, col_lists))
        flat_rows = products.reshape(N_SPACE, P_SIZE, OUT_BLOCKS * BLK)
        owned_part = flat_rows[:, :, :D_OWN].transpose(1, 0, 2).reshape(P_SIZE, N_DOF)
        interface = flat_rows[:, :, D_OWN:].transpose(1, 0, 2).reshape(P_SIZE, N_SPACE * IF_DEV)
        assembled = owned_part.at[:, global_row].add(interface, mode='drop')
        return assembled.astype(jnp.bfloat16)

    first_apply = one_apply(modes_in)
    second_apply = one_apply(first_apply)
    return (first_apply, second_apply)
```

```python
import functools

import jax
import jax.numpy as jnp
from jax import lax
from jax.experimental import pallas as pl
from jax.experimental.pallas import tpu as pltpu
from jax.sharding import PartitionSpec as P

MESH = pl.DeviceIdType.MESH
LANES = 128
MODE_GROUPS = 4
NT = (((1,), (1,)), ((), ()))


def kernel(
    n_space,
    modes_ref,
    blocks_hbm,
    cols_ref,
    send_ref,
    recv_ref,
    mix_cols_ref,
    mix_coef_ref,
    first_ref,
    second_ref,
    stiff,
    field,
    mixed,
    mixer_f32,
    mixer,
    pack_map,
    add_map,
    own_sum,
    outbox,
    inbox,
    load_sem,
    gather_send,
    gather_recv,
    swap_send,
    swap_recv,
):
    term_count, _, block_size, _ = stiff.shape
    _, chunk_count, _, mode_rows, chunk_dofs = field.shape
    modes_dev, owned_dofs = modes_ref.shape
    chunk_blocks = chunk_dofs // block_size
    owned_blocks = owned_dofs // block_size
    out_blocks = owned_blocks + send_ref.shape[1] // block_size
    stored = stiff.shape[1] // out_blocks
    slot_total = recv_ref.shape[1]
    cap = slot_total // n_space
    per_group = LANES // cap

    me = lax.axis_index("space")
    group = lax.axis_index("mode")
    sibling = group + 1 - 2 * lax.rem(group, 2)
    partner = lax.rem(group + 2, MODE_GROUPS)
    diagonal = lax.rem(sibling + 2, MODE_GROUPS)
    others = [lax.rem(me + step, n_space) for step in range(1, n_space)]

    barrier = pltpu.get_barrier_semaphore()
    pl.semaphore_signal(barrier, inc=1, device_id={"mode": partner}, device_id_type=MESH)
    pl.semaphore_signal(barrier, inc=1, device_id={"mode": sibling}, device_id_type=MESH)
    for other in others:
        pl.semaphore_signal(barrier, inc=1, device_id={"space": other}, device_id_type=MESH)

    loads = []
    edges = [(owned_blocks, out_blocks)]
    edges += [(c * chunk_blocks, (c + 1) * chunk_blocks) for c in range(chunk_count)]
    for at, (low, high) in enumerate(edges):
        span = pl.ds(low * stored, (high - low) * stored)
        load = pltpu.make_async_copy(blocks_hbm.at[:, span], stiff.at[:, span], load_sem.at[at])
        load.start()
        loads.append(load)

    for c in range(chunk_count):
        field[0, c, group, 16:mode_rows, :] = jnp.zeros((mode_rows - 16, chunk_dofs), jnp.bfloat16)
        field[0, c, group, 0:modes_dev, :] = modes_ref[:, c * chunk_dofs : (c + 1) * chunk_dofs]

    pl.semaphore_wait(barrier, n_space + 1)

    def gather_copy(apply, kind, c):
        owner = partner if kind == 2 else group
        target = partner if kind == 1 else sibling
        return pltpu.make_async_remote_copy(
            src_ref=field.at[apply, c, owner],
            dst_ref=field.at[apply, c, owner],
            send_sem=gather_send.at[apply, kind, c],
            recv_sem=gather_recv.at[apply, kind, c],
            device_id={"mode": target},
            device_id_type=MESH,
        )

    for c in range(chunk_count):
        gather_copy(0, 1, c).start()
    for c in range(chunk_count):
        gather_copy(0, 0, c).start()

    lane_rows = lax.broadcasted_iota(jnp.int32, (LANES, send_ref.shape[1]), 0)
    shifted = lane_rows - lax.rem(me, per_group) * cap
    position = jnp.where((shifted >= 0) & (shifted < cap), shifted, -slot_total - 1)
    slots = send_ref[...]
    for o in range(n_space):
        hit = position + o * cap == slots
        pack_map[o * LANES : (o + 1) * LANES, :] = jnp.where(hit, 1.0, 0.0).astype(jnp.bfloat16)

    rows = recv_ref[...]
    tall = 2 * LANES
    dof_ids = lax.broadcasted_iota(jnp.int32, (tall, slot_total), 0)
    for at in range(0, owned_dofs, tall):
        hit = dof_ids + at == rows
        add_map[at : at + tall, :] = jnp.where(hit, 1.0, 0.0).astype(jnp.bfloat16)

    mixer_f32[...] = jnp.zeros_like(mixer_f32)
    column_ids = lax.broadcasted_iota(jnp.int32, (modes_dev, LANES), 1)
    for k in range(term_count):
        columns = mix_cols_ref[k, 0:modes_dev, :]
        weights = mix_coef_ref[k, 0:modes_dev, :]
        for g in range(1, MODE_GROUPS):
            mine = group == g
            columns = jnp.where(mine, mix_cols_ref[k, g * modes_dev : (g + 1) * modes_dev, :], columns)
            weights = jnp.where(mine, mix_coef_ref[k, g * modes_dev : (g + 1) * modes_dev, :], weights)
        padded = columns
        for g in range(1, MODE_GROUPS + 1):
            padded = padded + jnp.where(columns >= g * modes_dev, mode_rows - modes_dev, 0)
        total = jnp.zeros((modes_dev, LANES), jnp.float32)
        for s in range(columns.shape[1]):
            total = total + jnp.where(padded[:, s : s + 1] == column_ids, weights[:, s : s + 1], 0.0)
        mixer_f32[k * mode_rows : k * mode_rows + modes_dev, :] = total
    mixer[...] = mixer_f32[...].astype(jnp.bfloat16)

    def row_product(c):
        picked = [
            mixed[cols_ref[c * stored + s], k * mode_rows : (k + 1) * mode_rows, :]
            for k in range(term_count)
            for s in range(stored)
        ]
        weights = stiff[:, c * stored : (c + 1) * stored].reshape(-1, block_size)
        return jnp.dot(jnp.concatenate(picked, axis=1), weights, preferred_element_type=jnp.float32)

    def swap_copy(apply, target):
        return pltpu.make_async_remote_copy(
            src_ref=outbox.at[apply, target],
            dst_ref=inbox.at[apply, me],
            send_sem=swap_send.at[apply, target],
            recv_sem=swap_recv.at[apply, me],
            device_id={"space": target},
            device_id_type=MESH,
        )

    def arrival(apply, source):
        return pltpu.make_async_remote_copy(
            src_ref=outbox.at[apply, source],
            dst_ref=inbox.at[apply, source],
            send_sem=swap_send.at[apply, source],
            recv_sem=swap_recv.at[apply, source],
            device_id={"space": source},
            device_id_type=MESH,
        )

    for apply, out_ref in enumerate((first_ref, second_ref)):
        for c in range(chunk_count):
            gather_copy(apply, 1, c).wait_recv()
            gather_copy(apply, 2, c).start()
        for c in range(chunk_count):
            gather_copy(apply, 0, c).wait_recv()
            gather_copy(apply, 2, c).wait_recv()
            whole = field[apply, c].reshape(MODE_GROUPS * mode_rows, chunk_dofs)
            product = jnp.dot(mixer[...], whole, preferred_element_type=jnp.float32)
            product = product.astype(jnp.bfloat16)
            for b in range(chunk_blocks):
                mixed[c * chunk_blocks + b] = product[:, b * block_size : (b + 1) * block_size]

        if apply == 0:
            loads[0].wait()
        interface = [row_product(c).astype(jnp.bfloat16) for c in range(owned_blocks, out_blocks)]
        packed = lax.dot_general(
            jnp.concatenate(interface, axis=1), pack_map[...], NT, preferred_element_type=jnp.float32
        ).astype(jnp.bfloat16)
        for o in range(n_space):
            outbox[apply, o] = packed[:, o * LANES : (o + 1) * LANES]
        for other in others:
            swap_copy(apply, other).start()
        inbox[apply, me] = outbox[apply, me]

        for c in range(chunk_count):
            if apply == 0:
                loads[1 + c].wait()
            for b in range(c * chunk_blocks, (c + 1) * chunk_blocks):
                own_sum[:, b * block_size : (b + 1) * block_size] = row_product(b)

        for other in others:
            arrival(apply, other).wait_recv()
        pieces = []
        for first in range(0, n_space, per_group):
            piece = inbox[apply, first]
            for source in range(first + 1, first + per_group):
                piece = piece + inbox[apply, source]
            pieces.append(piece)
        arrived = jnp.concatenate(pieces, axis=1)
        for c in range(chunk_count):
            span = slice(c * chunk_dofs, (c + 1) * chunk_dofs)
            added = lax.dot_general(arrived, add_map[span, :], NT, preferred_element_type=jnp.float32)
            result = (own_sum[:, span] + added).astype(jnp.bfloat16)
            if apply == 0:
                field[1, c, group] = result
                gather_copy(1, 1, c).start()
                gather_copy(1, 0, c).start()
            out_ref[:, span] = result[0:modes_dev, :]

    for apply in range(2):
        for c in range(chunk_count):
            for kind in range(3):
                gather_copy(apply, kind, c).wait_send()
        for other in others:
            swap_copy(apply, other).wait_send()


def local(n_space, modes_in, blocks, block_cols, send_slot, recv_row, mix_cols, mix_coef):
    modes_dev, owned_dofs = modes_in.shape
    term_count, block_total, block_size, _ = blocks.shape
    mode_rows = -(-modes_dev // 16) * 16
    chunk_dofs = 4 * block_size
    chunk_count = owned_dofs // chunk_dofs
    slot_total = recv_row.shape[0]
    interface_rows = send_slot.shape[0]
    vmem = pl.BlockSpec(memory_space=pltpu.VMEM)
    out = jax.ShapeDtypeStruct((modes_dev, owned_dofs), jnp.bfloat16)
    call = pl.pallas_call(
        functools.partial(kernel, n_space),
        out_shape=(out, out),
        in_specs=[
            vmem,
            pl.BlockSpec(memory_space=pl.ANY),
            pl.BlockSpec(memory_space=pltpu.SMEM),
            vmem,
            vmem,
            vmem,
            vmem,
        ],
        out_specs=(vmem, vmem),
        scratch_shapes=[
            pltpu.VMEM(blocks.shape, jnp.bfloat16),
            pltpu.VMEM((2, chunk_count, MODE_GROUPS, mode_rows, chunk_dofs), jnp.bfloat16),
            pltpu.VMEM((owned_dofs // block_size, term_count * mode_rows, block_size), jnp.bfloat16),
            pltpu.VMEM((term_count * mode_rows, LANES), jnp.float32),
            pltpu.VMEM((term_count * mode_rows, LANES), jnp.bfloat16),
            pltpu.VMEM((n_space * LANES, interface_rows), jnp.bfloat16),
            pltpu.VMEM((owned_dofs, slot_total), jnp.bfloat16),
            pltpu.VMEM((mode_rows, owned_dofs), jnp.float32),
            pltpu.VMEM((2, n_space, mode_rows, LANES), jnp.bfloat16),
            pltpu.VMEM((2, n_space, mode_rows, LANES), jnp.bfloat16),
            pltpu.SemaphoreType.DMA((1 + chunk_count,)),
            pltpu.SemaphoreType.DMA((2, 3, chunk_count)),
            pltpu.SemaphoreType.DMA((2, 3, chunk_count)),
            pltpu.SemaphoreType.DMA((2, n_space)),
            pltpu.SemaphoreType.DMA((2, n_space)),
        ],
        compiler_params=pltpu.CompilerParams(
            collective_id=0, has_side_effects=True, vmem_limit_bytes=56 * 1024 * 1024
        ),
    )
    return call(
        modes_in,
        blocks,
        block_cols.reshape(-1),
        send_slot.reshape(1, -1),
        recv_row.reshape(1, -1),
        mix_cols,
        mix_coef,
    )


def solution(mesh):
    in_specs = (
        P("mode", "space"),
        P(None, "space", None, None),
        P("space", None),
        P("space"),
        P("space"),
        P(),
        P(),
    )
    out_specs = (P("mode", "space"), P("mode", "space"))
    body = functools.partial(local, mesh.shape["space"])
    return jax.shard_map(body, mesh=mesh, in_specs=in_specs, out_specs=out_specs, check_vma=False)
```

```python
import functools

import jax
import jax.numpy as jnp
from jax import lax
from jax.experimental import pallas as pl
from jax.experimental.pallas import tpu as pltpu
from jax.sharding import PartitionSpec as P

MESH = pl.DeviceIdType.MESH
LANES = 128
MODE_GROUPS = 4
NT = (((1,), (1,)), ((), ()))


def kernel(
    n_space,
    modes_ref,
    blocks_hbm,
    cols_ref,
    send_ref,
    recv_ref,
    mix_cols_ref,
    mix_coef_ref,
    first_ref,
    second_ref,
    stiff,
    field,
    sums,
    arrived,
    mixed,
    turned,
    mixer_f32,
    mixer,
    pack_map,
    add_map,
    own_sum,
    outbox,
    inbox,
    load_sem,
    gather_send,
    gather_recv,
    swap_send,
    swap_recv,
):
    term_count, _, block_size, _ = stiff.shape
    chunk_count, _, mode_rows, chunk_dofs = field.shape
    modes_dev, owned_dofs = modes_ref.shape
    all_rows = MODE_GROUPS * mode_rows
    chunk_blocks = chunk_dofs // block_size
    owned_blocks = owned_dofs // block_size
    stored, out_blocks = cols_ref.shape
    slot_total = recv_ref.shape[1]
    cap = slot_total // n_space
    per_group = LANES // cap

    me = lax.axis_index("space")
    group = lax.axis_index("mode")
    sibling = group + 1 - 2 * lax.rem(group, 2)
    partner = lax.rem(group + 2, MODE_GROUPS)
    diagonal = lax.rem(sibling + 2, MODE_GROUPS)
    others = [lax.rem(me + step, n_space) for step in range(1, n_space)]

    barrier = pltpu.get_barrier_semaphore()
    pl.semaphore_signal(barrier, inc=1, device_id={"mode": partner}, device_id_type=MESH)
    pl.semaphore_signal(barrier, inc=1, device_id={"mode": sibling}, device_id_type=MESH)
    for other in others:
        pl.semaphore_signal(barrier, inc=1, device_id={"space": other}, device_id_type=MESH)

    chunk_slots = chunk_blocks * stored
    spans = [pl.ds(owned_blocks * stored, (out_blocks - owned_blocks) * stored)]
    for step in range(chunk_count):
        spans.append(pl.ds(lax.rem(group + step, chunk_count) * chunk_slots, chunk_slots))
    loads = [
        pltpu.make_async_copy(blocks_hbm.at[:, span], stiff.at[:, span], load_sem.at[at])
        for at, span in enumerate(spans)
    ]
    for load in loads:
        load.start()

    for c in range(chunk_count):
        field[c, group, 16:mode_rows, :] = jnp.zeros((mode_rows - 16, chunk_dofs), jnp.bfloat16)
        field[c, group, 0:modes_dev, :] = modes_ref[:, c * chunk_dofs : (c + 1) * chunk_dofs]

    pl.semaphore_wait(barrier, n_space + 1)

    def hop(view, kind, at):
        owner = partner if kind == 2 else group
        target = partner if kind == 1 else sibling
        return pltpu.make_async_remote_copy(
            src_ref=view(owner),
            dst_ref=view(owner),
            send_sem=gather_send.at[kind, at],
            recv_sem=gather_recv.at[kind, at],
            device_id={"mode": target},
            device_id_type=MESH,
        )

    def field_hop(kind, c):
        return hop(lambda owner: field.at[c, owner], kind, c)

    def sums_hop(kind, p):
        return hop(lambda owner: sums.at[owner, p], kind, chunk_count + p)

    def arrived_hop(kind):
        return hop(lambda owner: arrived.at[owner], kind, chunk_count + chunk_blocks)

    for c in range(chunk_count):
        field_hop(1, c).start()
    for c in range(chunk_count):
        field_hop(0, c).start()

    turned[...] = jnp.zeros_like(turned)
    mixer_f32[...] = jnp.zeros_like(mixer_f32)
    modes_all = mix_cols_ref.shape[2]
    row_ids = lax.broadcasted_iota(jnp.int32, (LANES, modes_all), 0)
    for k in range(term_count):
        columns = mix_cols_ref[k]
        weights = mix_coef_ref[k]
        padded = columns
        for g in range(1, MODE_GROUPS + 1):
            padded = padded + jnp.where(columns >= g * modes_dev, mode_rows - modes_dev, 0)
        total = jnp.zeros((LANES, modes_all), jnp.float32)
        for s in range(columns.shape[0]):
            total = total + jnp.where(padded[s : s + 1, :] == row_ids, weights[s : s + 1, :], 0.0)
        turned[k, :, 0:modes_all] = total
        by_mode = turned[k].T
        for g in range(MODE_GROUPS):
            mixer_f32[k, g, 0:modes_dev, :] = by_mode[g * modes_dev : (g + 1) * modes_dev, :]
    mixer[...] = mixer_f32[...].astype(jnp.bfloat16)

    lane_rows = lax.broadcasted_iota(jnp.int32, (LANES, send_ref.shape[1]), 0)
    shifted = lane_rows - lax.rem(me, per_group) * cap
    position = jnp.where((shifted >= 0) & (shifted < cap), shifted, -slot_total - 1)
    slots = send_ref[...]
    for o in range(n_space):
        hit = position + o * cap == slots
        pack_map[o * LANES : (o + 1) * LANES, :] = jnp.where(hit, 1.0, 0.0).astype(jnp.bfloat16)

    rows = recv_ref[...]
    tall = 2 * LANES
    dof_ids = lax.broadcasted_iota(jnp.int32, (tall, slot_total), 0)
    for at in range(0, owned_dofs, tall):
        hit = dof_ids + at == rows
        add_map[at : at + tall, :] = jnp.where(hit, 1.0, 0.0).astype(jnp.bfloat16)

    def row_weights(c):
        return stiff[:, pl.ds(c * stored, stored)].reshape(-1, block_size)

    def own_modes_row(c):
        picked = [mixed[cols_ref[s, c], k, group] for k in range(term_count) for s in range(stored)]
        return jnp.dot(jnp.concatenate(picked, axis=1), row_weights(c), preferred_element_type=jnp.float32)

    def all_modes_row(c):
        picked = [
            mixed[cols_ref[s, c], k].reshape(all_rows, block_size)
            for k in range(term_count)
            for s in range(stored)
        ]
        return jnp.dot(jnp.concatenate(picked, axis=1), row_weights(c), preferred_element_type=jnp.float32)

    def swap_copy(apply, target):
        return pltpu.make_async_remote_copy(
            src_ref=outbox.at[apply, target],
            dst_ref=inbox.at[apply, me],
            send_sem=swap_send.at[apply, target],
            recv_sem=swap_recv.at[apply, me],
            device_id={"space": target},
            device_id_type=MESH,
        )

    def arrival(apply, source):
        return pltpu.make_async_remote_copy(
            src_ref=outbox.at[apply, source],
            dst_ref=inbox.at[apply, source],
            send_sem=swap_send.at[apply, source],
            recv_sem=swap_recv.at[apply, source],
            device_id={"space": source},
            device_id_type=MESH,
        )

    def send_interface(apply):
        interface = [own_modes_row(c).astype(jnp.bfloat16) for c in range(owned_blocks, out_blocks)]
        packed = lax.dot_general(
            jnp.concatenate(interface, axis=1), pack_map[...], NT, preferred_element_type=jnp.float32
        ).astype(jnp.bfloat16)
        for o in range(n_space):
            outbox[apply, o] = packed[:, o * LANES : (o + 1) * LANES]
        for other in others:
            swap_copy(apply, other).start()
        inbox[apply, me] = outbox[apply, me]

    def take_interface(apply):
        for other in others:
            arrival(apply, other).wait_recv()
        pieces = []
        for first in range(0, n_space, per_group):
            piece = inbox[apply, first]
            for source in range(first + 1, first + per_group):
                piece = piece + inbox[apply, source]
            pieces.append(piece)
        return jnp.concatenate(pieces, axis=1)

    def mix_all(c):
        field_hop(0, c).wait_recv()
        field_hop(2, c).wait_recv()
        whole = field[c].reshape(all_rows, chunk_dofs)
        for k in range(term_count):
            product = jnp.dot(
                mixer[k].reshape(all_rows, LANES), whole, preferred_element_type=jnp.float32
            ).astype(jnp.bfloat16)
            product = product.reshape(MODE_GROUPS, mode_rows, chunk_dofs)
            for b in range(chunk_blocks):
                mixed[c * chunk_blocks + b, k] = product[:, :, b * block_size : (b + 1) * block_size]

    for c in range(chunk_count):
        field_hop(1, c).wait_recv()
        field_hop(2, c).start()
        if c > 0:
            mix_all(c - 1)
    mix_all(chunk_count - 1)

    loads[0].wait()
    send_interface(0)
    loads[1].wait()
    for p in range(chunk_blocks):
        sums[group, p] = all_modes_row(group * chunk_blocks + p).astype(jnp.bfloat16)
        sums_hop(1, p).start()
        sums_hop(0, p).start()
    early = chunk_blocks // 2
    for p in range(early):
        sums_hop(1, p).wait_recv()
        sums_hop(2, p).start()
    arrived[group] = take_interface(0)
    arrived_hop(1).start()
    arrived_hop(0).start()
    for p in range(early, chunk_blocks):
        sums_hop(1, p).wait_recv()
        sums_hop(2, p).start()
    arrived_hop(1).wait_recv()
    arrived_hop(2).start()
    arrived_hop(0).wait_recv()
    arrived_hop(2).wait_recv()

    arrived_all = arrived[...].reshape(all_rows, slot_total)
    own_mixer = mixer[:, group].reshape(term_count * mode_rows, LANES)
    for kind, c in ((None, group), (1, partner), (0, sibling), (2, diagonal)):
        if kind in (0, 2):
            for p in range(chunk_blocks):
                sums_hop(kind, p).wait_recv()
        at = pl.multiple_of(c * chunk_dofs, chunk_dofs)
        added = lax.dot_general(
            arrived_all, add_map[pl.ds(at, chunk_dofs), :], NT, preferred_element_type=jnp.float32
        )
        own = jnp.concatenate([sums[c, p] for p in range(chunk_blocks)], axis=1)
        whole = (own.astype(jnp.float32) + added).astype(jnp.bfloat16)
        own_sum[...] = whole.reshape(MODE_GROUPS, mode_rows, chunk_dofs)
        first_ref[:, pl.ds(at, chunk_dofs)] = own_sum[group, 0:modes_dev, :]
        product = jnp.dot(own_mixer, whole, preferred_element_type=jnp.float32).astype(jnp.bfloat16)
        product = product.reshape(term_count, mode_rows, chunk_dofs)
        for b in range(chunk_blocks):
            mixed[c * chunk_blocks + b, :, group] = product[:, :, b * block_size : (b + 1) * block_size]

    send_interface(1)
    for load in loads[2:]:
        load.wait()
    rows_now = [own_modes_row(c) for c in range(owned_blocks)]
    last_arrived = take_interface(1)
    for c in range(chunk_count):
        span = slice(c * chunk_dofs, (c + 1) * chunk_dofs)
        added = lax.dot_general(last_arrived, add_map[span, :], NT, preferred_element_type=jnp.float32)
        own = jnp.concatenate(rows_now[c * chunk_blocks : (c + 1) * chunk_blocks], axis=1)
        second_ref[:, span] = (own + added)[0:modes_dev, :].astype(jnp.bfloat16)

    for kind in range(3):
        for c in range(chunk_count):
            field_hop(kind, c).wait_send()
        for p in range(chunk_blocks):
            sums_hop(kind, p).wait_send()
        arrived_hop(kind).wait_send()
    for apply in range(2):
        for other in others:
            swap_copy(apply, other).wait_send()


def local(n_space, modes_in, blocks, block_cols, send_slot, recv_row, mix_cols, mix_coef):
    modes_dev, owned_dofs = modes_in.shape
    term_count, block_total, block_size, _ = blocks.shape
    mode_rows = -(-modes_dev // 16) * 16
    chunk_count = MODE_GROUPS
    chunk_dofs = owned_dofs // chunk_count
    chunk_blocks = chunk_dofs // block_size
    owned_blocks = owned_dofs // block_size
    slot_total = recv_row.shape[0]
    interface_rows = send_slot.shape[0]
    vmem = pl.BlockSpec(memory_space=pltpu.VMEM)
    out = jax.ShapeDtypeStruct((modes_dev, owned_dofs), jnp.bfloat16)
    call = pl.pallas_call(
        functools.partial(kernel, n_space),
        out_shape=(out, out),
        in_specs=[
            vmem,
            pl.BlockSpec(memory_space=pl.ANY),
            pl.BlockSpec(memory_space=pltpu.SMEM),
            vmem,
            vmem,
            vmem,
            vmem,
        ],
        out_specs=(vmem, vmem),
        scratch_shapes=[
            pltpu.VMEM(blocks.shape, jnp.bfloat16),
            pltpu.VMEM((chunk_count, MODE_GROUPS, mode_rows, chunk_dofs), jnp.bfloat16),
            pltpu.VMEM((chunk_count, chunk_blocks, MODE_GROUPS * mode_rows, block_size), jnp.bfloat16),
            pltpu.VMEM((MODE_GROUPS, mode_rows, slot_total), jnp.bfloat16),
            pltpu.VMEM((owned_blocks, term_count, MODE_GROUPS, mode_rows, block_size), jnp.bfloat16),
            pltpu.VMEM((term_count, LANES, LANES), jnp.float32),
            pltpu.VMEM((term_count, MODE_GROUPS, mode_rows, LANES), jnp.float32),
            pltpu.VMEM((term_count, MODE_GROUPS, mode_rows, LANES), jnp.bfloat16),
            pltpu.VMEM((n_space * LANES, interface_rows), jnp.bfloat16),
            pltpu.VMEM((owned_dofs, slot_total), jnp.bfloat16),
            pltpu.VMEM((MODE_GROUPS, mode_rows, chunk_dofs), jnp.bfloat16),
            pltpu.VMEM((2, n_space, mode_rows, LANES), jnp.bfloat16),
            pltpu.VMEM((2, n_space, mode_rows, LANES), jnp.bfloat16),
            pltpu.SemaphoreType.DMA((1 + chunk_count,)),
            pltpu.SemaphoreType.DMA((3, chunk_count + chunk_blocks + 1)),
            pltpu.SemaphoreType.DMA((3, chunk_count + chunk_blocks + 1)),
            pltpu.SemaphoreType.DMA((2, n_space)),
            pltpu.SemaphoreType.DMA((2, n_space)),
        ],
        compiler_params=pltpu.CompilerParams(
            collective_id=0, has_side_effects=True, vmem_limit_bytes=56 * 1024 * 1024
        ),
    )
    return call(
        modes_in,
        blocks,
        block_cols.T,
        send_slot.reshape(1, -1),
        recv_row.reshape(1, -1),
        mix_cols.transpose(0, 2, 1),
        mix_coef.transpose(0, 2, 1),
    )


def solution(mesh):
    in_specs = (
        P("mode", "space"),
        P(None, "space", None, None),
        P("space", None),
        P("space"),
        P("space"),
        P(),
        P(),
    )
    out_specs = (P("mode", "space"), P("mode", "space"))
    body = functools.partial(local, mesh.shape["space"])
    return jax.shard_map(body, mesh=mesh, in_specs=in_specs, out_specs=out_specs, check_vma=False)
```

```python
import functools

import jax
import jax.numpy as jnp
from jax import lax
from jax.experimental import pallas as pl
from jax.experimental.pallas import tpu as pltpu
from jax.sharding import PartitionSpec as P

MESH = pl.DeviceIdType.MESH
LANES = 128
MODE_GROUPS = 4


def kernel(
    n_space,
    modes_ref,
    blocks_hbm,
    cols_ref,
    send_ref,
    recv_ref,
    mix_cols_ref,
    mix_coef_ref,
    first_ref,
    second_ref,
    stiff,
    field,
    sums,
    arrived,
    mixed,
    turned,
    mixer_f32,
    mixer,
    pack_map,
    add_map,
    own_sum,
    outbox,
    inbox,
    load_sem,
    gather_send,
    gather_recv,
    swap_send,
    swap_recv,
):
    term_count, _, block_size, _ = stiff.shape
    chunk_count, _, mode_rows, chunk_dofs = field.shape
    modes_dev, owned_dofs = modes_ref.shape
    all_rows = MODE_GROUPS * mode_rows
    chunk_blocks = chunk_dofs // block_size
    owned_blocks = owned_dofs // block_size
    stored, out_blocks = cols_ref.shape
    slot_total = recv_ref.shape[1]
    cap = slot_total // n_space
    per_group = LANES // cap

    me = lax.axis_index("space")
    group = lax.axis_index("mode")
    sibling = group + 1 - 2 * lax.rem(group, 2)
    partner = lax.rem(group + 2, MODE_GROUPS)
    diagonal = lax.rem(sibling + 2, MODE_GROUPS)
    others = [lax.rem(me + step, n_space) for step in range(1, n_space)]

    barrier = pltpu.get_barrier_semaphore()
    pl.semaphore_signal(barrier, inc=1, device_id={"mode": partner}, device_id_type=MESH)
    pl.semaphore_signal(barrier, inc=1, device_id={"mode": sibling}, device_id_type=MESH)
    for other in others:
        pl.semaphore_signal(barrier, inc=1, device_id={"space": other}, device_id_type=MESH)

    chunk_slots = chunk_blocks * stored
    spans = [pl.ds(owned_blocks * stored, (out_blocks - owned_blocks) * stored)]
    for step in range(chunk_count):
        spans.append(pl.ds(lax.rem(group + step, chunk_count) * chunk_slots, chunk_slots))
    loads = [
        pltpu.make_async_copy(blocks_hbm.at[:, span], stiff.at[:, span], load_sem.at[at])
        for at, span in enumerate(spans)
    ]
    for load in loads:
        load.start()

    for c in range(chunk_count):
        field[c, group, 16:mode_rows, :] = jnp.zeros((mode_rows - 16, chunk_dofs), jnp.bfloat16)
        field[c, group, 0:modes_dev, :] = modes_ref[:, c * chunk_dofs : (c + 1) * chunk_dofs]

    pl.semaphore_wait(barrier, n_space + 1)

    def hop(view, kind, at):
        owner = partner if kind == 2 else group
        target = partner if kind == 1 else sibling
        return pltpu.make_async_remote_copy(
            src_ref=view(owner),
            dst_ref=view(owner),
            send_sem=gather_send.at[kind, at],
            recv_sem=gather_recv.at[kind, at],
            device_id={"mode": target},
            device_id_type=MESH,
        )

    def field_hop(kind, c):
        return hop(lambda owner: field.at[c, owner], kind, c)

    def sums_hop(kind, p):
        return hop(lambda owner: sums.at[owner, p], kind, chunk_count + p)

    def arrived_hop(kind):
        return hop(lambda owner: arrived.at[owner], kind, chunk_count + chunk_blocks)

    for c in range(chunk_count):
        field_hop(1, c).start()
    for c in range(chunk_count):
        field_hop(0, c).start()

    turned[...] = jnp.zeros_like(turned)
    mixer_f32[...] = jnp.zeros_like(mixer_f32)
    modes_all = mix_cols_ref.shape[2]
    row_ids = lax.broadcasted_iota(jnp.int32, (LANES, modes_all), 0)
    for k in range(term_count):
        columns = mix_cols_ref[k]
        weights = mix_coef_ref[k]
        padded = columns
        for g in range(1, MODE_GROUPS + 1):
            padded = padded + jnp.where(columns >= g * modes_dev, mode_rows - modes_dev, 0)
        total = jnp.zeros((LANES, modes_all), jnp.float32)
        for s in range(columns.shape[0]):
            total = total + jnp.where(padded[s : s + 1, :] == row_ids, weights[s : s + 1, :], 0.0)
        turned[k, :, 0:modes_all] = total
        by_mode = turned[k].T
        for g in range(MODE_GROUPS):
            mixer_f32[k, g, 0:modes_dev, :] = by_mode[g * modes_dev : (g + 1) * modes_dev, :]
    mixer[...] = mixer_f32[...].astype(jnp.bfloat16)

    def as_column(row):
        return jnp.broadcast_to(row.astype(jnp.float32), (LANES, LANES)).T.astype(jnp.int32)

    lanes = lax.broadcasted_iota(jnp.int32, (LANES, LANES), 1)
    shifted = lanes - lax.rem(me, per_group) * cap
    position = jnp.where((shifted >= 0) & (shifted < cap), shifted, -slot_total - 1)
    for at in range(0, send_ref.shape[1], LANES):
        slots = as_column(send_ref[:, at : at + LANES])
        for o in range(n_space):
            hit = position + o * cap == slots
            pack_map[at : at + LANES, o * LANES : (o + 1) * LANES] = jnp.where(hit, 1.0, 0.0).astype(jnp.bfloat16)
    for at in range(0, slot_total, LANES):
        rows = as_column(recv_ref[:, at : at + LANES])
        for b in range(owned_blocks):
            hit = lanes + b * LANES == rows
            add_map[at : at + LANES, b * LANES : (b + 1) * LANES] = jnp.where(hit, 1.0, 0.0).astype(jnp.bfloat16)

    def row_weights(c):
        return stiff[:, pl.ds(c * stored, stored)].reshape(-1, block_size)

    def own_modes_row(c):
        picked = [mixed[cols_ref[s, c], k, group] for k in range(term_count) for s in range(stored)]
        return jnp.dot(jnp.concatenate(picked, axis=1), row_weights(c), preferred_element_type=jnp.float32)

    def all_modes_row(c):
        picked = [
            mixed[cols_ref[s, c], k].reshape(all_rows, block_size)
            for k in range(term_count)
            for s in range(stored)
        ]
        return jnp.dot(jnp.concatenate(picked, axis=1), row_weights(c), preferred_element_type=jnp.float32)

    def swap_copy(apply, target):
        return pltpu.make_async_remote_copy(
            src_ref=outbox.at[apply, target],
            dst_ref=inbox.at[apply, me],
            send_sem=swap_send.at[apply, target],
            recv_sem=swap_recv.at[apply, me],
            device_id={"space": target},
            device_id_type=MESH,
        )

    def arrival(apply, source):
        return pltpu.make_async_remote_copy(
            src_ref=outbox.at[apply, source],
            dst_ref=inbox.at[apply, source],
            send_sem=swap_send.at[apply, source],
            recv_sem=swap_recv.at[apply, source],
            device_id={"space": source},
            device_id_type=MESH,
        )

    def send_interface(apply):
        interface = [own_modes_row(c).astype(jnp.bfloat16) for c in range(owned_blocks, out_blocks)]
        packed = jnp.dot(
            jnp.concatenate(interface, axis=1), pack_map[...], preferred_element_type=jnp.float32
        ).astype(jnp.bfloat16)
        for o in range(n_space):
            outbox[apply, o] = packed[:, o * LANES : (o + 1) * LANES]
        for other in others:
            swap_copy(apply, other).start()
        inbox[apply, me] = outbox[apply, me]

    def take_interface(apply):
        for other in others:
            arrival(apply, other).wait_recv()
        pieces = []
        for first in range(0, n_space, per_group):
            piece = inbox[apply, first]
            for source in range(first + 1, first + per_group):
                piece = piece + inbox[apply, source]
            pieces.append(piece)
        return jnp.concatenate(pieces, axis=1)

    def mix_all(c):
        field_hop(0, c).wait_recv()
        field_hop(2, c).wait_recv()
        whole = field[c].reshape(all_rows, chunk_dofs)
        for k in range(term_count):
            product = jnp.dot(
                mixer[k].reshape(all_rows, LANES), whole, preferred_element_type=jnp.float32
            ).astype(jnp.bfloat16)
            product = product.reshape(MODE_GROUPS, mode_rows, chunk_dofs)
            for b in range(chunk_blocks):
                mixed[c * chunk_blocks + b, k] = product[:, :, b * block_size : (b + 1) * block_size]

    for c in range(chunk_count):
        field_hop(1, c).wait_recv()
        field_hop(2, c).start()
        if c > 0:
            mix_all(c - 1)
    mix_all(chunk_count - 1)

    loads[0].wait()
    send_interface(0)
    loads[1].wait()
    for p in range(chunk_blocks):
        sums[group, p] = all_modes_row(group * chunk_blocks + p).astype(jnp.bfloat16)
        sums_hop(1, p).start()
        sums_hop(0, p).start()
    early = chunk_blocks // 2
    for p in range(early):
        sums_hop(1, p).wait_recv()
        sums_hop(2, p).start()
    arrived[group] = take_interface(0)
    arrived_hop(1).start()
    arrived_hop(0).start()
    for p in range(early, chunk_blocks):
        sums_hop(1, p).wait_recv()
        sums_hop(2, p).start()
    arrived_hop(1).wait_recv()
    arrived_hop(2).start()
    arrived_hop(0).wait_recv()
    arrived_hop(2).wait_recv()

    arrived_all = arrived[...].reshape(all_rows, slot_total)
    own_mixer = mixer[:, group].reshape(term_count * mode_rows, LANES)
    for kind, c in ((None, group), (1, partner), (0, sibling), (2, diagonal)):
        if kind in (0, 2):
            for p in range(chunk_blocks):
                sums_hop(kind, p).wait_recv()
        at = pl.multiple_of(c * chunk_dofs, chunk_dofs)
        added = jnp.dot(
            arrived_all, add_map[:, pl.ds(at, chunk_dofs)], preferred_element_type=jnp.float32
        )
        own = jnp.concatenate([sums[c, p] for p in range(chunk_blocks)], axis=1)
        whole = (own.astype(jnp.float32) + added).astype(jnp.bfloat16)
        own_sum[...] = whole.reshape(MODE_GROUPS, mode_rows, chunk_dofs)
        first_ref[:, pl.ds(at, chunk_dofs)] = own_sum[group, 0:modes_dev, :]
        product = jnp.dot(own_mixer, whole, preferred_element_type=jnp.float32).astype(jnp.bfloat16)
        product = product.reshape(term_count, mode_rows, chunk_dofs)
        for b in range(chunk_blocks):
            mixed[c * chunk_blocks + b, :, group] = product[:, :, b * block_size : (b + 1) * block_size]

    send_interface(1)
    for load in loads[2:]:
        load.wait()
    rows_now = [own_modes_row(c) for c in range(owned_blocks)]
    last_arrived = take_interface(1)
    for c in range(chunk_count):
        span = slice(c * chunk_dofs, (c + 1) * chunk_dofs)
        added = jnp.dot(last_arrived, add_map[:, span], preferred_element_type=jnp.float32)
        own = jnp.concatenate(rows_now[c * chunk_blocks : (c + 1) * chunk_blocks], axis=1)
        second_ref[:, span] = (own + added)[0:modes_dev, :].astype(jnp.bfloat16)

    for kind in range(3):
        for c in range(chunk_count):
            field_hop(kind, c).wait_send()
        for p in range(chunk_blocks):
            sums_hop(kind, p).wait_send()
        arrived_hop(kind).wait_send()
    for apply in range(2):
        for other in others:
            swap_copy(apply, other).wait_send()


def hand_over(first_in, second_in, first_out, second_out, sem):
    first = pltpu.make_async_copy(first_in, first_out, sem.at[0])
    second = pltpu.make_async_copy(second_in, second_out, sem.at[1])
    first.start()
    second.start()
    first.wait()
    second.wait()


def local(n_space, modes_in, blocks, block_cols, send_slot, recv_row, mix_cols, mix_coef):
    modes_dev, owned_dofs = modes_in.shape
    term_count, block_total, block_size, _ = blocks.shape
    mode_rows = -(-modes_dev // 16) * 16
    chunk_count = MODE_GROUPS
    chunk_dofs = owned_dofs // chunk_count
    chunk_blocks = chunk_dofs // block_size
    owned_blocks = owned_dofs // block_size
    slot_total = recv_row.shape[0]
    interface_rows = send_slot.shape[0]
    vmem = pl.BlockSpec(memory_space=pltpu.VMEM)
    out = jax.ShapeDtypeStruct((modes_dev, owned_dofs), jnp.bfloat16)
    call = pl.pallas_call(
        functools.partial(kernel, n_space),
        out_shape=(out, out),
        in_specs=[
            vmem,
            pl.BlockSpec(memory_space=pltpu.HBM),
            pl.BlockSpec(memory_space=pltpu.SMEM),
            vmem,
            vmem,
            vmem,
            vmem,
        ],
        out_specs=(vmem, vmem),
        scratch_shapes=[
            pltpu.VMEM(blocks.shape, jnp.bfloat16),
            pltpu.VMEM((chunk_count, MODE_GROUPS, mode_rows, chunk_dofs), jnp.bfloat16),
            pltpu.VMEM((chunk_count, chunk_blocks, MODE_GROUPS * mode_rows, block_size), jnp.bfloat16),
            pltpu.VMEM((MODE_GROUPS, mode_rows, slot_total), jnp.bfloat16),
            pltpu.VMEM((owned_blocks, term_count, MODE_GROUPS, mode_rows, block_size), jnp.bfloat16),
            pltpu.VMEM((term_count, LANES, LANES), jnp.float32),
            pltpu.VMEM((term_count, MODE_GROUPS, mode_rows, LANES), jnp.float32),
            pltpu.VMEM((term_count, MODE_GROUPS, mode_rows, LANES), jnp.bfloat16),
            pltpu.VMEM((interface_rows, n_space * LANES), jnp.bfloat16),
            pltpu.VMEM((slot_total, owned_dofs), jnp.bfloat16),
            pltpu.VMEM((MODE_GROUPS, mode_rows, chunk_dofs), jnp.bfloat16),
            pltpu.VMEM((2, n_space, mode_rows, LANES), jnp.bfloat16),
            pltpu.VMEM((2, n_space, mode_rows, LANES), jnp.bfloat16),
            pltpu.SemaphoreType.DMA((1 + chunk_count,)),
            pltpu.SemaphoreType.DMA((3, chunk_count + chunk_blocks + 1)),
            pltpu.SemaphoreType.DMA((3, chunk_count + chunk_blocks + 1)),
            pltpu.SemaphoreType.DMA((2, n_space)),
            pltpu.SemaphoreType.DMA((2, n_space)),
        ],
        compiler_params=pltpu.CompilerParams(
            collective_id=0, has_side_effects=True, vmem_limit_bytes=53 * 1024 * 1024
        ),
    )
    results = call(
        modes_in,
        blocks,
        block_cols.T,
        send_slot.reshape(1, -1),
        recv_row.reshape(1, -1),
        mix_cols.transpose(0, 2, 1),
        mix_coef.transpose(0, 2, 1),
    )
    anywhere = pl.BlockSpec(memory_space=pl.ANY)
    return pl.pallas_call(
        hand_over,
        out_shape=(out, out),
        in_specs=[anywhere, anywhere],
        out_specs=(anywhere, anywhere),
        scratch_shapes=[pltpu.SemaphoreType.DMA((2,))],
    )(*results)


def solution(mesh):
    in_specs = (
        P("mode", "space"),
        P(None, "space", None, None),
        P("space", None),
        P("space"),
        P("space"),
        P(),
        P(),
    )
    out_specs = (P("mode", "space"), P("mode", "space"))
    body = functools.partial(local, mesh.shape["space"])
    return jax.shard_map(body, mesh=mesh, in_specs=in_specs, out_specs=out_specs, check_vma=False)
```

```python
import functools

import jax
import jax.numpy as jnp
from jax import lax
from jax.experimental import pallas as pl
from jax.experimental.pallas import tpu as pltpu
from jax.sharding import PartitionSpec as P

MESH = pl.DeviceIdType.MESH
LANES = 128
MODE_GROUPS = 4


def kernel(
    n_space,
    modes_ref,
    blocks_hbm,
    cols_ref,
    send_ref,
    recv_ref,
    mix_cols_ref,
    mix_coef_ref,
    out_ref,
    stiff,
    field,
    sums,
    arrived,
    mixed,
    turned,
    mixer_f32,
    mixer,
    pack_map,
    add_map,
    own_sum,
    outbox,
    inbox,
    load_sem,
    gather_send,
    gather_recv,
    swap_send,
    swap_recv,
):
    term_count, _, block_size, _ = stiff.shape
    chunk_count, _, mode_rows, chunk_dofs = field.shape
    modes_dev, owned_dofs = modes_ref.shape
    all_rows = MODE_GROUPS * mode_rows
    chunk_blocks = chunk_dofs // block_size
    owned_blocks = owned_dofs // block_size
    stored, out_blocks = cols_ref.shape
    slot_total = recv_ref.shape[1]
    cap = slot_total // n_space
    per_group = LANES // cap

    me = lax.axis_index("space")
    group = lax.axis_index("mode")
    sibling = group + 1 - 2 * lax.rem(group, 2)
    partner = lax.rem(group + 2, MODE_GROUPS)
    diagonal = lax.rem(sibling + 2, MODE_GROUPS)
    others = [lax.rem(me + step, n_space) for step in range(1, n_space)]

    barrier = pltpu.get_barrier_semaphore()
    pl.semaphore_signal(barrier, inc=1, device_id={"mode": partner}, device_id_type=MESH)
    pl.semaphore_signal(barrier, inc=1, device_id={"mode": sibling}, device_id_type=MESH)
    for other in others:
        pl.semaphore_signal(barrier, inc=1, device_id={"space": other}, device_id_type=MESH)

    chunk_slots = chunk_blocks * stored
    spans = [pl.ds(owned_blocks * stored, (out_blocks - owned_blocks) * stored)]
    for step in range(chunk_count):
        spans.append(pl.ds(lax.rem(group + step, chunk_count) * chunk_slots, chunk_slots))
    loads = [
        pltpu.make_async_copy(blocks_hbm.at[:, span], stiff.at[:, span], load_sem.at[at])
        for at, span in enumerate(spans)
    ]
    for load in loads:
        load.start()

    for c in range(chunk_count):
        field[c, group, 16:mode_rows, :] = jnp.zeros((mode_rows - 16, chunk_dofs), jnp.bfloat16)
        field[c, group, 0:modes_dev, :] = modes_ref[:, c * chunk_dofs : (c + 1) * chunk_dofs]

    pl.semaphore_wait(barrier, n_space + 1)

    def hop(view, kind, at):
        owner = partner if kind == 2 else group
        target = partner if kind == 1 else sibling
        return pltpu.make_async_remote_copy(
            src_ref=view(owner),
            dst_ref=view(owner),
            send_sem=gather_send.at[kind, at],
            recv_sem=gather_recv.at[kind, at],
            device_id={"mode": target},
            device_id_type=MESH,
        )

    def field_hop(kind, c):
        return hop(lambda owner: field.at[c, owner], kind, c)

    def sums_hop(kind, p):
        return hop(lambda owner: sums.at[owner, p], kind, chunk_count + p)

    def arrived_hop(kind):
        return hop(lambda owner: arrived.at[owner], kind, chunk_count + chunk_blocks)

    for c in range(chunk_count):
        field_hop(1, c).start()
    for c in range(chunk_count):
        field_hop(0, c).start()

    turned[...] = jnp.zeros_like(turned)
    mixer_f32[...] = jnp.zeros_like(mixer_f32)
    modes_all = mix_cols_ref.shape[2]
    row_ids = lax.broadcasted_iota(jnp.int32, (LANES, modes_all), 0)
    for k in range(term_count):
        columns = mix_cols_ref[k]
        weights = mix_coef_ref[k]
        padded = columns
        for g in range(1, MODE_GROUPS + 1):
            padded = padded + jnp.where(columns >= g * modes_dev, mode_rows - modes_dev, 0)
        total = jnp.zeros((LANES, modes_all), jnp.float32)
        for s in range(columns.shape[0]):
            total = total + jnp.where(padded[s : s + 1, :] == row_ids, weights[s : s + 1, :], 0.0)
        turned[k, :, 0:modes_all] = total
        by_mode = turned[k].T
        for g in range(MODE_GROUPS):
            mixer_f32[k, g, 0:modes_dev, :] = by_mode[g * modes_dev : (g + 1) * modes_dev, :]
    mixer[...] = mixer_f32[...].astype(jnp.bfloat16)

    def as_column(row):
        return jnp.broadcast_to(row.astype(jnp.float32), (LANES, LANES)).T.astype(jnp.int32)

    lanes = lax.broadcasted_iota(jnp.int32, (LANES, LANES), 1)
    shifted = lanes - lax.rem(me, per_group) * cap
    position = jnp.where((shifted >= 0) & (shifted < cap), shifted, -slot_total - 1)
    for at in range(0, send_ref.shape[1], LANES):
        slots = as_column(send_ref[:, at : at + LANES])
        for o in range(n_space):
            hit = position + o * cap == slots
            pack_map[at : at + LANES, o * LANES : (o + 1) * LANES] = jnp.where(hit, 1.0, 0.0).astype(jnp.bfloat16)
    for at in range(0, slot_total, LANES):
        rows = as_column(recv_ref[:, at : at + LANES])
        for b in range(owned_blocks):
            hit = lanes + b * LANES == rows
            add_map[at : at + LANES, b * LANES : (b + 1) * LANES] = jnp.where(hit, 1.0, 0.0).astype(jnp.bfloat16)

    def row_weights(c):
        return stiff[:, pl.ds(c * stored, stored)].reshape(-1, block_size)

    def own_modes_pair(c):
        picked = [
            jnp.concatenate(
                [mixed[cols_ref[s, r], k, group] for k in range(term_count) for s in range(stored)], axis=1
            )
            for r in (c, c + 1)
        ]
        weights = jnp.concatenate([row_weights(c), row_weights(c + 1)], axis=1)
        product = jnp.dot(jnp.concatenate(picked, axis=0), weights, preferred_element_type=jnp.float32)
        return jnp.concatenate(
            [product[:mode_rows, :block_size], product[mode_rows:, block_size:]], axis=1
        )

    def all_modes_row(c):
        picked = [
            mixed[cols_ref[s, c], k].reshape(all_rows, block_size)
            for k in range(term_count)
            for s in range(stored)
        ]
        return jnp.dot(jnp.concatenate(picked, axis=1), row_weights(c), preferred_element_type=jnp.float32)

    def swap_copy(apply, target):
        return pltpu.make_async_remote_copy(
            src_ref=outbox.at[apply, target],
            dst_ref=inbox.at[apply, me],
            send_sem=swap_send.at[apply, target],
            recv_sem=swap_recv.at[apply, me],
            device_id={"space": target},
            device_id_type=MESH,
        )

    def arrival(apply, source):
        return pltpu.make_async_remote_copy(
            src_ref=outbox.at[apply, source],
            dst_ref=inbox.at[apply, source],
            send_sem=swap_send.at[apply, source],
            recv_sem=swap_recv.at[apply, source],
            device_id={"space": source},
            device_id_type=MESH,
        )

    def send_interface(apply):
        interface = [own_modes_pair(c).astype(jnp.bfloat16) for c in range(owned_blocks, out_blocks, 2)]
        packed = jnp.dot(
            jnp.concatenate(interface, axis=1), pack_map[...], preferred_element_type=jnp.float32
        ).astype(jnp.bfloat16)
        for o in range(n_space):
            outbox[apply, o] = packed[:, o * LANES : (o + 1) * LANES]
        for other in others:
            swap_copy(apply, other).start()
        inbox[apply, me] = outbox[apply, me]

    def take_interface(apply):
        for other in others:
            arrival(apply, other).wait_recv()
        pieces = []
        for first in range(0, n_space, per_group):
            piece = inbox[apply, first]
            for source in range(first + 1, first + per_group):
                piece = piece + inbox[apply, source]
            pieces.append(piece)
        return jnp.concatenate(pieces, axis=1)

    def mix_all(c):
        field_hop(0, c).wait_recv()
        field_hop(2, c).wait_recv()
        whole = field[c].reshape(all_rows, chunk_dofs)
        product = jnp.dot(
            mixer[...].reshape(term_count * all_rows, LANES), whole, preferred_element_type=jnp.float32
        ).astype(jnp.bfloat16)
        product = product.reshape(term_count, MODE_GROUPS, mode_rows, chunk_dofs)
        for b in range(chunk_blocks):
            mixed[c * chunk_blocks + b] = product[..., b * block_size : (b + 1) * block_size]

    for c in range(chunk_count):
        field_hop(1, c).wait_recv()
        field_hop(2, c).start()
        if c > 0:
            mix_all(c - 1)
    mix_all(chunk_count - 1)

    loads[0].wait()
    send_interface(0)
    loads[1].wait()
    for p in range(chunk_blocks):
        sums[group, p] = all_modes_row(group * chunk_blocks + p).astype(jnp.bfloat16)
        sums_hop(1, p).start()
        sums_hop(0, p).start()
    early = chunk_blocks // 2
    for p in range(early):
        sums_hop(1, p).wait_recv()
        sums_hop(2, p).start()
    arrived[group] = take_interface(0)
    arrived_hop(1).start()
    arrived_hop(0).start()
    for p in range(early, chunk_blocks):
        sums_hop(1, p).wait_recv()
        sums_hop(2, p).start()
    arrived_hop(1).wait_recv()
    arrived_hop(2).start()
    arrived_hop(0).wait_recv()
    arrived_hop(2).wait_recv()

    arrived_all = arrived[...].reshape(all_rows, slot_total)
    own_mixer = mixer[:, group].reshape(term_count * mode_rows, LANES)
    for kind, c in ((None, group), (1, partner), (0, sibling), (2, diagonal)):
        if kind in (0, 2):
            for p in range(chunk_blocks):
                sums_hop(kind, p).wait_recv()
        at = pl.multiple_of(c * chunk_dofs, chunk_dofs)
        added = jnp.dot(
            arrived_all, add_map[:, pl.ds(at, chunk_dofs)], preferred_element_type=jnp.float32
        )
        own = jnp.concatenate([sums[c, p] for p in range(chunk_blocks)], axis=1)
        whole = (own.astype(jnp.float32) + added).astype(jnp.bfloat16)
        own_sum[...] = whole.reshape(MODE_GROUPS, mode_rows, chunk_dofs)
        out_ref[0, :, pl.ds(at, chunk_dofs)] = own_sum[group, 0:modes_dev, :]
        product = jnp.dot(own_mixer, whole, preferred_element_type=jnp.float32).astype(jnp.bfloat16)
        product = product.reshape(term_count, mode_rows, chunk_dofs)
        for b in range(chunk_blocks):
            mixed[c * chunk_blocks + b, :, group] = product[:, :, b * block_size : (b + 1) * block_size]

    send_interface(1)
    for load in loads[2:]:
        load.wait()
    rows_now = [own_modes_pair(c) for c in range(0, owned_blocks, 2)]
    last_arrived = take_interface(1)
    for c in range(chunk_count):
        span = slice(c * chunk_dofs, (c + 1) * chunk_dofs)
        added = jnp.dot(last_arrived, add_map[:, span], preferred_element_type=jnp.float32)
        own = jnp.concatenate(rows_now[c * chunk_blocks // 2 : (c + 1) * chunk_blocks // 2], axis=1)
        out_ref[1, :, span] = (own + added)[0:modes_dev, :].astype(jnp.bfloat16)

    for kind in range(3):
        for c in range(chunk_count):
            field_hop(kind, c).wait_send()
        for p in range(chunk_blocks):
            sums_hop(kind, p).wait_send()
        arrived_hop(kind).wait_send()
    for apply in range(2):
        for other in others:
            swap_copy(apply, other).wait_send()


def local(n_space, modes_in, blocks, block_cols, send_slot, recv_row, mix_cols, mix_coef):
    modes_dev, owned_dofs = modes_in.shape
    term_count, block_total, block_size, _ = blocks.shape
    mode_rows = -(-modes_dev // 16) * 16
    chunk_count = MODE_GROUPS
    chunk_dofs = owned_dofs // chunk_count
    chunk_blocks = chunk_dofs // block_size
    owned_blocks = owned_dofs // block_size
    slot_total = recv_row.shape[0]
    interface_rows = send_slot.shape[0]
    vmem = pl.BlockSpec(memory_space=pltpu.VMEM)
    out = jax.ShapeDtypeStruct((2, modes_dev, owned_dofs), jnp.bfloat16)
    call = pl.pallas_call(
        functools.partial(kernel, n_space),
        out_shape=out,
        in_specs=[
            vmem,
            pl.BlockSpec(memory_space=pltpu.HBM),
            pl.BlockSpec(memory_space=pltpu.SMEM),
            vmem,
            vmem,
            vmem,
            vmem,
        ],
        out_specs=vmem,
        scratch_shapes=[
            pltpu.VMEM(blocks.shape, jnp.bfloat16),
            pltpu.VMEM((chunk_count, MODE_GROUPS, mode_rows, chunk_dofs), jnp.bfloat16),
            pltpu.VMEM((chunk_count, chunk_blocks, MODE_GROUPS * mode_rows, block_size), jnp.bfloat16),
            pltpu.VMEM((MODE_GROUPS, mode_rows, slot_total), jnp.bfloat16),
            pltpu.VMEM((owned_blocks, term_count, MODE_GROUPS, mode_rows, block_size), jnp.bfloat16),
            pltpu.VMEM((term_count, LANES, LANES), jnp.float32),
            pltpu.VMEM((term_count, MODE_GROUPS, mode_rows, LANES), jnp.float32),
            pltpu.VMEM((term_count, MODE_GROUPS, mode_rows, LANES), jnp.bfloat16),
            pltpu.VMEM((interface_rows, n_space * LANES), jnp.bfloat16),
            pltpu.VMEM((slot_total, owned_dofs), jnp.bfloat16),
            pltpu.VMEM((MODE_GROUPS, mode_rows, chunk_dofs), jnp.bfloat16),
            pltpu.VMEM((2, n_space, mode_rows, LANES), jnp.bfloat16),
            pltpu.VMEM((2, n_space, mode_rows, LANES), jnp.bfloat16),
            pltpu.SemaphoreType.DMA((1 + chunk_count,)),
            pltpu.SemaphoreType.DMA((3, chunk_count + chunk_blocks + 1)),
            pltpu.SemaphoreType.DMA((3, chunk_count + chunk_blocks + 1)),
            pltpu.SemaphoreType.DMA((2, n_space)),
            pltpu.SemaphoreType.DMA((2, n_space)),
        ],
        compiler_params=pltpu.CompilerParams(
            collective_id=0, has_side_effects=True, vmem_limit_bytes=56 * 1024 * 1024
        ),
    )
    results = call(
        modes_in,
        blocks,
        block_cols.T,
        send_slot.reshape(1, -1),
        recv_row.reshape(1, -1),
        mix_cols.transpose(0, 2, 1),
        mix_coef.transpose(0, 2, 1),
    )

    return results[0], results[1]


def solution(mesh):
    in_specs = (
        P("mode", "space"),
        P(None, "space", None, None),
        P("space", None),
        P("space"),
        P("space"),
        P(),
        P(),
    )
    out_specs = (P("mode", "space"), P("mode", "space"))
    body = functools.partial(local, mesh.shape["space"])
    return jax.shard_map(body, mesh=mesh, in_specs=in_specs, out_specs=out_specs, check_vma=False)
```

```python
import functools

import jax
import jax.numpy as jnp
from jax import lax
from jax.experimental import pallas as pl
from jax.experimental.pallas import tpu as pltpu
from jax.sharding import PartitionSpec as P

MESH = pl.DeviceIdType.MESH
LANES = 128
MODE_GROUPS = 4


def kernel(
    n_space,
    modes_ref,
    blocks_hbm,
    cols_ref,
    send_ref,
    recv_ref,
    mix_cols_ref,
    mix_coef_ref,
    out_ref,
    stiff,
    field,
    sums,
    arrived,
    mixed,
    turned,
    mixer_f32,
    mixer,
    pack_map,
    add_map,
    own_sum,
    outbox,
    inbox,
    load_sem,
    gather_send,
    gather_recv,
    swap_send,
    swap_recv,
):
    term_count, _, block_size, _ = stiff.shape
    chunk_count, _, mode_rows, chunk_dofs = field.shape
    modes_dev, owned_dofs = modes_ref.shape
    all_rows = MODE_GROUPS * mode_rows
    chunk_blocks = chunk_dofs // block_size
    owned_blocks = owned_dofs // block_size
    stored, out_blocks = cols_ref.shape
    slot_total = recv_ref.shape[1]
    cap = slot_total // n_space
    half_lanes = LANES // 2
    per_half = half_lanes // cap
    half_blocks = owned_blocks // 2

    me = lax.axis_index("space")
    group = lax.axis_index("mode")
    sibling = group + 1 - 2 * lax.rem(group, 2)
    partner = lax.rem(group + 2, MODE_GROUPS)
    half = lax.rem(group, 2)
    others = [lax.rem(me + step, n_space) for step in range(1, n_space)]

    barrier = pltpu.get_barrier_semaphore()
    pl.semaphore_signal(barrier, inc=1, device_id={"mode": partner}, device_id_type=MESH)
    pl.semaphore_signal(barrier, inc=1, device_id={"mode": sibling}, device_id_type=MESH)
    for other in others:
        pl.semaphore_signal(barrier, inc=1, device_id={"space": other}, device_id_type=MESH)

    half_slots = half_blocks * stored
    spans = [pl.ds(owned_blocks * stored, (out_blocks - owned_blocks) * stored)]
    spans += [pl.ds(at * half_slots, half_slots) for at in (half, 1 - half)]
    loads = [
        pltpu.make_async_copy(blocks_hbm.at[:, span], stiff.at[:, span], load_sem.at[at])
        for at, span in enumerate(spans)
    ]
    for load in loads:
        load.start()

    for c in range(chunk_count):
        field[c, group, 16:mode_rows, :] = jnp.zeros((mode_rows - 16, chunk_dofs), jnp.bfloat16)
        field[c, group, 0:modes_dev, :] = modes_ref[:, c * chunk_dofs : (c + 1) * chunk_dofs]

    pl.semaphore_wait(barrier, n_space + 1)

    def hop(view, kind, at):
        owner = partner if kind == 2 else group
        target = partner if kind == 1 else sibling
        return pltpu.make_async_remote_copy(
            src_ref=view(owner),
            dst_ref=view(owner),
            send_sem=gather_send.at[kind, at],
            recv_sem=gather_recv.at[kind, at],
            device_id={"mode": target},
            device_id_type=MESH,
        )

    def field_hop(kind, c):
        return hop(lambda owner: field.at[c, owner], kind, c)

    def sums_hop(p):
        return hop(lambda owner: sums.at[half, p], 0, chunk_count + p)

    def arrived_hop():
        return hop(lambda owner: arrived.at[half], 0, chunk_count + half_blocks)

    for c in range(chunk_count):
        field_hop(1, c).start()
    for c in range(chunk_count):
        field_hop(0, c).start()

    turned[...] = jnp.zeros_like(turned)
    mixer_f32[...] = jnp.zeros_like(mixer_f32)
    modes_all = mix_cols_ref.shape[2]
    row_ids = lax.broadcasted_iota(jnp.int32, (LANES, modes_all), 0)
    for k in range(term_count):
        columns = mix_cols_ref[k]
        weights = mix_coef_ref[k]
        padded = columns
        for g in range(1, MODE_GROUPS + 1):
            padded = padded + jnp.where(columns >= g * modes_dev, mode_rows - modes_dev, 0)
        total = jnp.zeros((LANES, modes_all), jnp.float32)
        for s in range(columns.shape[0]):
            total = total + jnp.where(padded[s : s + 1, :] == row_ids, weights[s : s + 1, :], 0.0)
        turned[k, :, 0:modes_all] = total
        by_mode = turned[k].T
        for g in range(MODE_GROUPS):
            mixer_f32[k, g, 0:modes_dev, :] = by_mode[g * modes_dev : (g + 1) * modes_dev, :]
    mixer[...] = mixer_f32[...].astype(jnp.bfloat16)

    def as_column(row):
        return jnp.broadcast_to(row.astype(jnp.float32), (LANES, LANES)).T.astype(jnp.int32)

    lanes = lax.broadcasted_iota(jnp.int32, (LANES, LANES), 1)
    interface_rows = send_ref.shape[1]
    for side in range(2):
        shifted = lanes - lax.rem(me, per_half) * cap - side * half_lanes
        position = jnp.where((shifted >= 0) & (shifted < cap), shifted, -slot_total - 1)
        for at in range(0, interface_rows, LANES):
            slots = as_column(send_ref[:, at : at + LANES])
            low = side * interface_rows + at
            for o in range(n_space):
                hit = position + o * cap == slots
                pack_map[low : low + LANES, o * LANES : (o + 1) * LANES] = jnp.where(hit, 1.0, 0.0).astype(
                    jnp.bfloat16
                )
    for at in range(0, slot_total, LANES):
        rows = as_column(recv_ref[:, at : at + LANES])
        for b in range(owned_blocks):
            hit = lanes + b * LANES == rows
            add_map[at : at + LANES, b * LANES : (b + 1) * LANES] = jnp.where(hit, 1.0, 0.0).astype(jnp.bfloat16)

    def row_weights(c):
        return stiff[:, pl.ds(c * stored, stored)].reshape(-1, block_size)

    def own_modes(column, k):
        return mixed[column, k, group]

    def half_modes(column, k):
        return mixed[column, k, pl.ds(2 * half, 2)].reshape(2 * mode_rows, block_size)

    def pair_product(c, modes):
        picked = [
            jnp.concatenate([modes(cols_ref[s, r], k) for k in range(term_count) for s in range(stored)], axis=1)
            for r in (c, c + 1)
        ]
        weights = jnp.concatenate([row_weights(c), row_weights(c + 1)], axis=1)
        product = jnp.dot(jnp.concatenate(picked, axis=0), weights, preferred_element_type=jnp.float32)
        tall = product.shape[0] // 2
        return jnp.concatenate([product[:tall, :block_size], product[tall:, block_size:]], axis=1)

    def all_modes_row(c):
        picked = [
            mixed[cols_ref[s, c], k].reshape(all_rows, block_size)
            for k in range(term_count)
            for s in range(stored)
        ]
        return jnp.dot(jnp.concatenate(picked, axis=1), row_weights(c), preferred_element_type=jnp.float32)

    def swap_copy(apply, target):
        return pltpu.make_async_remote_copy(
            src_ref=outbox.at[apply, target],
            dst_ref=inbox.at[apply, me],
            send_sem=swap_send.at[apply, target],
            recv_sem=swap_recv.at[apply, me],
            device_id={"space": target},
            device_id_type=MESH,
        )

    def arrival(apply, source):
        return pltpu.make_async_remote_copy(
            src_ref=outbox.at[apply, source],
            dst_ref=inbox.at[apply, source],
            send_sem=swap_send.at[apply, source],
            recv_sem=swap_recv.at[apply, source],
            device_id={"space": source},
            device_id_type=MESH,
        )

    def send_interface(apply):
        modes = half_modes if apply == 0 else own_modes
        interface = jnp.concatenate(
            [pair_product(c, modes).astype(jnp.bfloat16) for c in range(owned_blocks, out_blocks, 2)], axis=1
        )
        if apply == 0:
            interface = jnp.concatenate([interface[:mode_rows], interface[mode_rows:]], axis=1)
        packed = jnp.dot(
            interface, pack_map[0 : interface.shape[1], :], preferred_element_type=jnp.float32
        ).astype(jnp.bfloat16)
        for o in range(n_space):
            outbox[apply, o] = packed[:, o * LANES : (o + 1) * LANES]
        for other in others:
            swap_copy(apply, other).start()
        inbox[apply, me] = outbox[apply, me]

    def take_interface(apply):
        for other in others:
            arrival(apply, other).wait_recv()
        pieces = []
        for first in range(0, n_space, per_half):
            piece = inbox[apply, first].astype(jnp.float32)
            for source in range(first + 1, first + per_half):
                piece = piece + inbox[apply, source].astype(jnp.float32)
            pieces.append(piece)
        left = lax.broadcasted_iota(jnp.int32, (mode_rows, LANES), 1) < half_lanes
        low, high = [], []
        for even, odd in zip(pieces[0::2], pieces[1::2]):
            low.append(jnp.where(left, even, pltpu.roll(odd, half_lanes, 1)))
            high.append(jnp.where(left, pltpu.roll(even, half_lanes, 1), odd))
        low = jnp.concatenate(low, axis=1).astype(jnp.bfloat16)
        if apply == 1:
            return low
        return jnp.concatenate([low, jnp.concatenate(high, axis=1).astype(jnp.bfloat16)], axis=0)

    def mix_all(c):
        field_hop(0, c).wait_recv()
        field_hop(2, c).wait_recv()
        whole = field[c].reshape(all_rows, chunk_dofs)
        product = jnp.dot(
            mixer[...].reshape(term_count * all_rows, LANES), whole, preferred_element_type=jnp.float32
        ).astype(jnp.bfloat16)
        product = product.reshape(term_count, MODE_GROUPS, mode_rows, chunk_dofs)
        for b in range(chunk_blocks):
            mixed[c * chunk_blocks + b] = product[..., b * block_size : (b + 1) * block_size]

    for c in range(chunk_count):
        field_hop(1, c).wait_recv()
        field_hop(2, c).start()
        if c > 0:
            mix_all(c - 1)
    mix_all(chunk_count - 1)

    loads[0].wait()
    send_interface(0)
    loads[1].wait()
    for p in range(half_blocks):
        sums[half, p] = all_modes_row(half * half_blocks + p).astype(jnp.bfloat16)
        sums_hop(p).start()
    arrived[half] = take_interface(0)
    arrived_hop().start()
    for p in range(half_blocks):
        sums_hop(p).wait_recv()
    arrived_hop().wait_recv()

    arrived_all = arrived[...].reshape(all_rows, slot_total)
    own_mixer = mixer[:, group].reshape(term_count * mode_rows, LANES)
    for c in range(chunk_count):
        span = slice(c * chunk_dofs, (c + 1) * chunk_dofs)
        added = jnp.dot(arrived_all, add_map[:, span], preferred_element_type=jnp.float32)
        blocks_now = range(c * chunk_blocks, (c + 1) * chunk_blocks)
        own = jnp.concatenate([sums[b // half_blocks, b % half_blocks] for b in blocks_now], axis=1)
        whole = (own.astype(jnp.float32) + added).astype(jnp.bfloat16)
        own_sum[...] = whole.reshape(MODE_GROUPS, mode_rows, chunk_dofs)
        out_ref[0, :, span] = own_sum[group, 0:modes_dev, :]
        product = jnp.dot(own_mixer, whole, preferred_element_type=jnp.float32).astype(jnp.bfloat16)
        product = product.reshape(term_count, mode_rows, chunk_dofs)
        for b in range(chunk_blocks):
            mixed[c * chunk_blocks + b, :, group] = product[:, :, b * block_size : (b + 1) * block_size]

    send_interface(1)
    for load in loads[2:]:
        load.wait()
    rows_now = [pair_product(c, own_modes) for c in range(0, owned_blocks, 2)]
    last_arrived = take_interface(1)
    for c in range(chunk_count):
        span = slice(c * chunk_dofs, (c + 1) * chunk_dofs)
        added = jnp.dot(last_arrived, add_map[:, span], preferred_element_type=jnp.float32)
        own = jnp.concatenate(rows_now[c * chunk_blocks // 2 : (c + 1) * chunk_blocks // 2], axis=1)
        out_ref[1, :, span] = (own + added)[0:modes_dev, :].astype(jnp.bfloat16)

    for kind in range(3):
        for c in range(chunk_count):
            field_hop(kind, c).wait_send()
    for p in range(half_blocks):
        sums_hop(p).wait_send()
    arrived_hop().wait_send()
    for apply in range(2):
        for other in others:
            swap_copy(apply, other).wait_send()


def local(n_space, modes_in, blocks, block_cols, send_slot, recv_row, mix_cols, mix_coef):
    modes_dev, owned_dofs = modes_in.shape
    term_count, block_total, block_size, _ = blocks.shape
    mode_rows = -(-modes_dev // 16) * 16
    chunk_count = MODE_GROUPS
    chunk_dofs = owned_dofs // chunk_count
    owned_blocks = owned_dofs // block_size
    slot_total = recv_row.shape[0]
    interface_rows = send_slot.shape[0]
    vmem = pl.BlockSpec(memory_space=pltpu.VMEM)
    out = jax.ShapeDtypeStruct((2, modes_dev, owned_dofs), jnp.bfloat16)
    call = pl.pallas_call(
        functools.partial(kernel, n_space),
        out_shape=out,
        in_specs=[
            vmem,
            pl.BlockSpec(memory_space=pltpu.HBM),
            pl.BlockSpec(memory_space=pltpu.SMEM),
            vmem,
            vmem,
            vmem,
            vmem,
        ],
        out_specs=vmem,
        scratch_shapes=[
            pltpu.VMEM(blocks.shape, jnp.bfloat16),
            pltpu.VMEM((chunk_count, MODE_GROUPS, mode_rows, chunk_dofs), jnp.bfloat16),
            pltpu.VMEM((2, owned_blocks // 2, MODE_GROUPS * mode_rows, block_size), jnp.bfloat16),
            pltpu.VMEM((2, 2 * mode_rows, slot_total), jnp.bfloat16),
            pltpu.VMEM((owned_blocks, term_count, MODE_GROUPS, mode_rows, block_size), jnp.bfloat16),
            pltpu.VMEM((term_count, LANES, LANES), jnp.float32),
            pltpu.VMEM((term_count, MODE_GROUPS, mode_rows, LANES), jnp.float32),
            pltpu.VMEM((term_count, MODE_GROUPS, mode_rows, LANES), jnp.bfloat16),
            pltpu.VMEM((2 * interface_rows, n_space * LANES), jnp.bfloat16),
            pltpu.VMEM((slot_total, owned_dofs), jnp.bfloat16),
            pltpu.VMEM((MODE_GROUPS, mode_rows, chunk_dofs), jnp.bfloat16),
            pltpu.VMEM((2, n_space, mode_rows, LANES), jnp.bfloat16),
            pltpu.VMEM((2, n_space, mode_rows, LANES), jnp.bfloat16),
            pltpu.SemaphoreType.DMA((3,)),
            pltpu.SemaphoreType.DMA((3, chunk_count + owned_blocks // 2 + 1)),
            pltpu.SemaphoreType.DMA((3, chunk_count + owned_blocks // 2 + 1)),
            pltpu.SemaphoreType.DMA((2, n_space)),
            pltpu.SemaphoreType.DMA((2, n_space)),
        ],
        compiler_params=pltpu.CompilerParams(
            collective_id=0, has_side_effects=True, vmem_limit_bytes=56 * 1024 * 1024
        ),
    )
    results = call(
        modes_in,
        blocks,
        block_cols.T,
        send_slot.reshape(1, -1),
        recv_row.reshape(1, -1),
        mix_cols.transpose(0, 2, 1),
        mix_coef.transpose(0, 2, 1),
    )

    return results[0], results[1]


def solution(mesh):
    in_specs = (
        P("mode", "space"),
        P(None, "space", None, None),
        P("space", None),
        P("space"),
        P("space"),
        P(),
        P(),
    )
    out_specs = (P("mode", "space"), P("mode", "space"))
    body = functools.partial(local, mesh.shape["space"])
    return jax.shard_map(body, mesh=mesh, in_specs=in_specs, out_specs=out_specs, check_vma=False)
```

```python
import functools

import jax
import jax.numpy as jnp
from jax import lax
from jax.experimental import pallas as pl
from jax.experimental.pallas import tpu as pltpu
from jax.sharding import PartitionSpec as P

MESH = pl.DeviceIdType.MESH
LANES = 128
MODE_GROUPS = 4


def kernel(
    n_space,
    modes_ref,
    blocks_hbm,
    cols_ref,
    send_ref,
    recv_ref,
    mix_cols_ref,
    mix_coef_ref,
    out_ref,
    stiff,
    field,
    sums,
    arrived,
    mixed,
    turned,
    mixer_f32,
    mixer,
    pack_map,
    add_map,
    own_mixed,
    outbox,
    inbox,
    load_sem,
    gather_send,
    gather_recv,
    swap_send,
    swap_recv,
):
    term_count, _, block_size, _ = stiff.shape
    chunk_count, _, mode_rows, chunk_dofs = field.shape
    modes_dev, owned_dofs = modes_ref.shape
    all_rows = MODE_GROUPS * mode_rows
    chunk_blocks = chunk_dofs // block_size
    owned_blocks = owned_dofs // block_size
    stored, out_blocks = cols_ref.shape
    slot_total = recv_ref.shape[1]
    cap = slot_total // n_space
    half_lanes = LANES // 2
    per_half = half_lanes // cap
    half_blocks = owned_blocks // 2

    me = lax.axis_index("space")
    group = lax.axis_index("mode")
    sibling = group + 1 - 2 * lax.rem(group, 2)
    partner = lax.rem(group + 2, MODE_GROUPS)
    half = lax.rem(group, 2)
    others = [lax.rem(me + step, n_space) for step in range(1, n_space)]

    barrier = pltpu.get_barrier_semaphore()
    pl.semaphore_signal(barrier, inc=1, device_id={"mode": partner}, device_id_type=MESH)
    pl.semaphore_signal(barrier, inc=1, device_id={"mode": sibling}, device_id_type=MESH)
    for other in others:
        pl.semaphore_signal(barrier, inc=1, device_id={"space": other}, device_id_type=MESH)

    half_slots = half_blocks * stored
    spans = [pl.ds(owned_blocks * stored, (out_blocks - owned_blocks) * stored)]
    spans += [pl.ds(at * half_slots, half_slots) for at in (half, 1 - half)]
    loads = [
        pltpu.make_async_copy(blocks_hbm.at[:, span], stiff.at[:, span], load_sem.at[at])
        for at, span in enumerate(spans)
    ]
    for load in loads:
        load.start()

    for c in range(chunk_count):
        field[c, group, 16:mode_rows, :] = jnp.zeros((mode_rows - 16, chunk_dofs), jnp.bfloat16)
        field[c, group, 0:modes_dev, :] = modes_ref[:, c * chunk_dofs : (c + 1) * chunk_dofs]

    pl.semaphore_wait(barrier, n_space + 1)

    def hop(view, kind, at):
        owner = partner if kind == 2 else group
        target = partner if kind == 1 else sibling
        return pltpu.make_async_remote_copy(
            src_ref=view(owner),
            dst_ref=view(owner),
            send_sem=gather_send.at[kind, at],
            recv_sem=gather_recv.at[kind, at],
            device_id={"mode": target},
            device_id_type=MESH,
        )

    def field_hop(kind, c):
        return hop(lambda owner: field.at[c, owner], kind, c)

    def sums_hop(p):
        return hop(lambda owner: sums.at[half, p], 0, chunk_count + p)

    def arrived_hop():
        return hop(lambda owner: arrived.at[half], 0, chunk_count + half_blocks)

    for c in range(chunk_count):
        field_hop(1, c).start()
    for c in range(chunk_count):
        field_hop(0, c).start()

    turned[...] = jnp.zeros_like(turned)
    mixer_f32[...] = jnp.zeros_like(mixer_f32)
    modes_all = mix_cols_ref.shape[2]
    row_ids = lax.broadcasted_iota(jnp.int32, (LANES, modes_all), 0)
    for k in range(term_count):
        columns = mix_cols_ref[k]
        weights = mix_coef_ref[k]
        padded = columns
        for g in range(1, MODE_GROUPS + 1):
            padded = padded + jnp.where(columns >= g * modes_dev, mode_rows - modes_dev, 0)
        total = jnp.zeros((LANES, modes_all), jnp.float32)
        for s in range(columns.shape[0]):
            total = total + jnp.where(padded[s : s + 1, :] == row_ids, weights[s : s + 1, :], 0.0)
        turned[k, :, 0:modes_all] = total
        by_mode = turned[k].T
        for g in range(MODE_GROUPS):
            mixer_f32[k, g, 0:modes_dev, :] = by_mode[g * modes_dev : (g + 1) * modes_dev, :]
    mixer[...] = mixer_f32[...].astype(jnp.bfloat16)

    def as_column(row):
        return jnp.broadcast_to(row.astype(jnp.float32), (LANES, LANES)).T.astype(jnp.int32)

    lanes = lax.broadcasted_iota(jnp.int32, (LANES, LANES), 1)
    interface_rows = send_ref.shape[1]
    for side in range(2):
        shifted = lanes - lax.rem(me, per_half) * cap - side * half_lanes
        position = jnp.where((shifted >= 0) & (shifted < cap), shifted, -slot_total - 1)
        for at in range(0, interface_rows, LANES):
            slots = as_column(send_ref[:, at : at + LANES])
            low = side * interface_rows + at
            for o in range(n_space):
                hit = position + o * cap == slots
                pack_map[low : low + LANES, o * LANES : (o + 1) * LANES] = jnp.where(hit, 1.0, 0.0).astype(
                    jnp.bfloat16
                )
    for at in range(0, slot_total, LANES):
        rows = as_column(recv_ref[:, at : at + LANES])
        for b in range(owned_blocks):
            hit = lanes + b * LANES == rows
            add_map[at : at + LANES, b * LANES : (b + 1) * LANES] = jnp.where(hit, 1.0, 0.0).astype(jnp.bfloat16)

    def row_weights(c):
        return stiff[:, pl.ds(c * stored, stored)].reshape(-1, block_size)

    def own_modes(column, k):
        return mixed[column, k, group]

    def half_modes(column, k):
        return mixed[column, k, pl.ds(2 * half, 2)].reshape(2 * mode_rows, block_size)

    def pair_product(c, modes):
        picked = [
            jnp.concatenate([modes(cols_ref[s, r], k) for k in range(term_count) for s in range(stored)], axis=1)
            for r in (c, c + 1)
        ]
        weights = jnp.concatenate([row_weights(c), row_weights(c + 1)], axis=1)
        product = jnp.dot(jnp.concatenate(picked, axis=0), weights, preferred_element_type=jnp.float32)
        tall = product.shape[0] // 2
        return jnp.concatenate([product[:tall, :block_size], product[tall:, block_size:]], axis=1)

    def all_modes_row(c):
        picked = [
            mixed[cols_ref[s, c], k].reshape(all_rows, block_size)
            for k in range(term_count)
            for s in range(stored)
        ]
        return jnp.dot(jnp.concatenate(picked, axis=1), row_weights(c), preferred_element_type=jnp.float32)

    def swap_copy(apply, target):
        return pltpu.make_async_remote_copy(
            src_ref=outbox.at[apply, target],
            dst_ref=inbox.at[apply, me],
            send_sem=swap_send.at[apply, target],
            recv_sem=swap_recv.at[apply, me],
            device_id={"space": target},
            device_id_type=MESH,
        )

    def arrival(apply, source):
        return pltpu.make_async_remote_copy(
            src_ref=outbox.at[apply, source],
            dst_ref=inbox.at[apply, source],
            send_sem=swap_send.at[apply, source],
            recv_sem=swap_recv.at[apply, source],
            device_id={"space": source},
            device_id_type=MESH,
        )

    def send_interface(apply):
        modes = half_modes if apply == 0 else own_modes
        interface = jnp.concatenate(
            [pair_product(c, modes).astype(jnp.bfloat16) for c in range(owned_blocks, out_blocks, 2)], axis=1
        )
        if apply == 0:
            interface = jnp.concatenate([interface[:mode_rows], interface[mode_rows:]], axis=1)
        packed = jnp.dot(
            interface, pack_map[0 : interface.shape[1], :], preferred_element_type=jnp.float32
        ).astype(jnp.bfloat16)
        for o in range(n_space):
            outbox[apply, o] = packed[:, o * LANES : (o + 1) * LANES]
        for other in others:
            swap_copy(apply, other).start()
        inbox[apply, me] = outbox[apply, me]

    def take_interface(apply):
        for other in others:
            arrival(apply, other).wait_recv()
        pieces = []
        for first in range(0, n_space, per_half):
            piece = inbox[apply, first].astype(jnp.float32)
            for source in range(first + 1, first + per_half):
                piece = piece + inbox[apply, source].astype(jnp.float32)
            pieces.append(piece)
        left = lax.broadcasted_iota(jnp.int32, (mode_rows, LANES), 1) < half_lanes
        low, high = [], []
        for even, odd in zip(pieces[0::2], pieces[1::2]):
            low.append(jnp.where(left, even, pltpu.roll(odd, half_lanes, 1)))
            high.append(jnp.where(left, pltpu.roll(even, half_lanes, 1), odd))
        low = jnp.concatenate(low, axis=1).astype(jnp.bfloat16)
        if apply == 1:
            return low
        return jnp.concatenate([low, jnp.concatenate(high, axis=1).astype(jnp.bfloat16)], axis=0)

    def mix_all(c):
        field_hop(0, c).wait_recv()
        field_hop(2, c).wait_recv()
        whole = field[c].reshape(all_rows, chunk_dofs)
        product = jnp.dot(
            mixer[...].reshape(term_count * all_rows, LANES), whole, preferred_element_type=jnp.float32
        ).astype(jnp.bfloat16)
        product = product.reshape(term_count, MODE_GROUPS, mode_rows, chunk_dofs)
        for b in range(chunk_blocks):
            mixed[c * chunk_blocks + b] = product[..., b * block_size : (b + 1) * block_size]

    for c in range(chunk_count):
        field_hop(1, c).wait_recv()
        field_hop(2, c).start()
        if c > 0:
            mix_all(c - 1)
    mix_all(chunk_count - 1)

    loads[0].wait()
    send_interface(0)
    loads[1].wait()
    for p in range(half_blocks):
        sums[half, p] = all_modes_row(half * half_blocks + p).astype(jnp.bfloat16)
        sums_hop(p).start()
    own_mixer = mixer[:, group].reshape(term_count * mode_rows, LANES)
    for p in range(half_blocks):
        sums_hop(p).wait_recv()
    for c in range(chunk_count):
        blocks_now = range(c * chunk_blocks, (c + 1) * chunk_blocks)
        own = jnp.concatenate([sums[b // half_blocks, b % half_blocks] for b in blocks_now], axis=1)
        own_mixed[c] = jnp.dot(own_mixer, own, preferred_element_type=jnp.float32)
    arrived[half] = take_interface(0).reshape(2, mode_rows, slot_total)
    arrived_hop().start()
    arrived_hop().wait_recv()

    arrived_all = arrived[...].reshape(all_rows, slot_total)
    arrived_mixed = jnp.dot(own_mixer, arrived_all, preferred_element_type=jnp.float32).astype(jnp.bfloat16)
    for c in range(chunk_count):
        span = slice(c * chunk_dofs, (c + 1) * chunk_dofs)
        added = jnp.dot(arrived_mixed, add_map[:, span], preferred_element_type=jnp.float32)
        product = (own_mixed[c] + added).astype(jnp.bfloat16)
        product = product.reshape(term_count, mode_rows, chunk_dofs)
        for b in range(chunk_blocks):
            mixed[c * chunk_blocks + b, :, group] = product[:, :, b * block_size : (b + 1) * block_size]

    send_interface(1)
    own_at = pl.ds(pl.multiple_of(group * mode_rows, mode_rows), mode_rows)
    own_arrived = arrived[group // 2, half]
    for c in range(chunk_count):
        span = slice(c * chunk_dofs, (c + 1) * chunk_dofs)
        added = jnp.dot(own_arrived, add_map[:, span], preferred_element_type=jnp.float32)
        blocks_now = range(c * chunk_blocks, (c + 1) * chunk_blocks)
        own = jnp.concatenate([sums[b // half_blocks, b % half_blocks, own_at, :] for b in blocks_now], axis=1)
        out_ref[0, :, span] = (own.astype(jnp.float32) + added)[0:modes_dev, :].astype(jnp.bfloat16)
    for load in loads[2:]:
        load.wait()
    rows_now = [pair_product(c, own_modes) for c in range(0, owned_blocks, 2)]
    last_arrived = take_interface(1)
    for c in range(chunk_count):
        span = slice(c * chunk_dofs, (c + 1) * chunk_dofs)
        added = jnp.dot(last_arrived, add_map[:, span], preferred_element_type=jnp.float32)
        own = jnp.concatenate(rows_now[c * chunk_blocks // 2 : (c + 1) * chunk_blocks // 2], axis=1)
        out_ref[1, :, span] = (own + added)[0:modes_dev, :].astype(jnp.bfloat16)

    for kind in range(3):
        for c in range(chunk_count):
            field_hop(kind, c).wait_send()
    for p in range(half_blocks):
        sums_hop(p).wait_send()
    arrived_hop().wait_send()
    for apply in range(2):
        for other in others:
            swap_copy(apply, other).wait_send()


def local(n_space, modes_in, blocks, block_cols, send_slot, recv_row, mix_cols, mix_coef):
    modes_dev, owned_dofs = modes_in.shape
    term_count, block_total, block_size, _ = blocks.shape
    mode_rows = -(-modes_dev // 16) * 16
    chunk_count = MODE_GROUPS
    chunk_dofs = owned_dofs // chunk_count
    owned_blocks = owned_dofs // block_size
    slot_total = recv_row.shape[0]
    interface_rows = send_slot.shape[0]
    vmem = pl.BlockSpec(memory_space=pltpu.VMEM)
    out = jax.ShapeDtypeStruct((2, modes_dev, owned_dofs), jnp.bfloat16)
    call = pl.pallas_call(
        functools.partial(kernel, n_space),
        out_shape=out,
        in_specs=[
            vmem,
            pl.BlockSpec(memory_space=pltpu.HBM),
            pl.BlockSpec(memory_space=pltpu.SMEM),
            vmem,
            vmem,
            vmem,
            vmem,
        ],
        out_specs=vmem,
        scratch_shapes=[
            pltpu.VMEM(blocks.shape, jnp.bfloat16),
            pltpu.VMEM((chunk_count, MODE_GROUPS, mode_rows, chunk_dofs), jnp.bfloat16),
            pltpu.VMEM((2, owned_blocks // 2, MODE_GROUPS * mode_rows, block_size), jnp.bfloat16),
            pltpu.VMEM((2, 2, mode_rows, slot_total), jnp.bfloat16),
            pltpu.VMEM((owned_blocks, term_count, MODE_GROUPS, mode_rows, block_size), jnp.bfloat16),
            pltpu.VMEM((term_count, LANES, LANES), jnp.float32),
            pltpu.VMEM((term_count, MODE_GROUPS, mode_rows, LANES), jnp.float32),
            pltpu.VMEM((term_count, MODE_GROUPS, mode_rows, LANES), jnp.bfloat16),
            pltpu.VMEM((2 * interface_rows, n_space * LANES), jnp.bfloat16),
            pltpu.VMEM((slot_total, owned_dofs), jnp.bfloat16),
            pltpu.VMEM((chunk_count, term_count * mode_rows, chunk_dofs), jnp.float32),
            pltpu.VMEM((2, n_space, mode_rows, LANES), jnp.bfloat16),
            pltpu.VMEM((2, n_space, mode_rows, LANES), jnp.bfloat16),
            pltpu.SemaphoreType.DMA((3,)),
            pltpu.SemaphoreType.DMA((3, chunk_count + owned_blocks // 2 + 1)),
            pltpu.SemaphoreType.DMA((3, chunk_count + owned_blocks // 2 + 1)),
            pltpu.SemaphoreType.DMA((2, n_space)),
            pltpu.SemaphoreType.DMA((2, n_space)),
        ],
        compiler_params=pltpu.CompilerParams(
            collective_id=0, has_side_effects=True, vmem_limit_bytes=56 * 1024 * 1024
        ),
    )
    results = call(
        modes_in,
        blocks,
        block_cols.T,
        send_slot.reshape(1, -1),
        recv_row.reshape(1, -1),
        mix_cols.transpose(0, 2, 1),
        mix_coef.transpose(0, 2, 1),
    )

    return results[0], results[1]


def solution(mesh):
    in_specs = (
        P("mode", "space"),
        P(None, "space", None, None),
        P("space", None),
        P("space"),
        P("space"),
        P(),
        P(),
    )
    out_specs = (P("mode", "space"), P("mode", "space"))
    body = functools.partial(local, mesh.shape["space"])
    return jax.shard_map(body, mesh=mesh, in_specs=in_specs, out_specs=out_specs, check_vma=False)
```

```python
import functools

import jax
import jax.numpy as jnp
from jax import lax
from jax.experimental import pallas as pl
from jax.experimental.pallas import tpu as pltpu
from jax.sharding import PartitionSpec as P

MESH = pl.DeviceIdType.MESH
LANES = 128
MODE_GROUPS = 4


def kernel(
    n_space,
    modes_ref,
    blocks_hbm,
    cols_ref,
    send_ref,
    recv_ref,
    mix_cols_ref,
    mix_coef_ref,
    out_ref,
    stiff,
    field,
    sums,
    arrived,
    mixed,
    turned,
    mixer_f32,
    mixer,
    pack_map,
    add_map,
    own_mixed,
    outbox,
    inbox,
    load_sem,
    gather_send,
    gather_recv,
    swap_send,
    swap_recv,
):
    term_count, _, block_size, _ = stiff.shape
    chunk_count, _, mode_rows, chunk_dofs = field.shape
    modes_dev, owned_dofs = modes_ref.shape
    all_rows = MODE_GROUPS * mode_rows
    chunk_blocks = chunk_dofs // block_size
    owned_blocks = owned_dofs // block_size
    stored, out_blocks = cols_ref.shape
    slot_total = recv_ref.shape[1]
    cap = slot_total // n_space
    half_lanes = LANES // 2
    per_half = half_lanes // cap
    half_blocks = owned_blocks // 2

    me = lax.axis_index("space")
    group = lax.axis_index("mode")
    sibling = group + 1 - 2 * lax.rem(group, 2)
    partner = lax.rem(group + 2, MODE_GROUPS)
    half = lax.rem(group, 2)
    others = [lax.rem(me + step, n_space) for step in range(1, n_space)]

    barrier = pltpu.get_barrier_semaphore()
    pl.semaphore_signal(barrier, inc=1, device_id={"mode": partner}, device_id_type=MESH)
    pl.semaphore_signal(barrier, inc=1, device_id={"mode": sibling}, device_id_type=MESH)
    for other in others:
        pl.semaphore_signal(barrier, inc=1, device_id={"space": other}, device_id_type=MESH)

    half_slots = half_blocks * stored
    spans = [pl.ds(owned_blocks * stored, (out_blocks - owned_blocks) * stored)]
    spans += [pl.ds(at * half_slots, half_slots) for at in (half, 1 - half)]
    loads = [
        pltpu.make_async_copy(blocks_hbm.at[:, span], stiff.at[:, span], load_sem.at[at])
        for at, span in enumerate(spans)
    ]
    for load in loads:
        load.start()

    for c in range(chunk_count):
        field[c, group, 16:mode_rows, :] = jnp.zeros((mode_rows - 16, chunk_dofs), jnp.bfloat16)
        field[c, group, 0:modes_dev, :] = modes_ref[:, c * chunk_dofs : (c + 1) * chunk_dofs]

    pl.semaphore_wait(barrier, n_space + 1)

    def hop(view, kind, at):
        owner = partner if kind == 2 else group
        target = partner if kind == 1 else sibling
        return pltpu.make_async_remote_copy(
            src_ref=view(owner),
            dst_ref=view(owner),
            send_sem=gather_send.at[kind, at],
            recv_sem=gather_recv.at[kind, at],
            device_id={"mode": target},
            device_id_type=MESH,
        )

    def field_hop(kind, c):
        return hop(lambda owner: field.at[c, owner], kind, c)

    def sums_hop(p):
        return hop(lambda owner: sums.at[half, p], 0, chunk_count + p)

    def arrived_hop():
        return hop(lambda owner: arrived.at[half], 0, chunk_count + half_blocks)

    for c in range(chunk_count):
        field_hop(1, c).start()
    for c in range(chunk_count):
        field_hop(0, c).start()

    turned[...] = jnp.zeros_like(turned)
    mixer_f32[...] = jnp.zeros_like(mixer_f32)
    modes_all = mix_cols_ref.shape[2]
    row_ids = lax.broadcasted_iota(jnp.int32, (LANES, modes_all), 0)
    for k in range(term_count):
        columns = mix_cols_ref[k]
        weights = mix_coef_ref[k]
        padded = columns
        for g in range(1, MODE_GROUPS + 1):
            padded = padded + jnp.where(columns >= g * modes_dev, mode_rows - modes_dev, 0)
        total = jnp.zeros((LANES, modes_all), jnp.float32)
        for s in range(columns.shape[0]):
            total = total + jnp.where(padded[s : s + 1, :] == row_ids, weights[s : s + 1, :], 0.0)
        turned[k, :, 0:modes_all] = total
        by_mode = turned[k].T
        for g in range(MODE_GROUPS):
            mixer_f32[k, g, 0:modes_dev, :] = by_mode[g * modes_dev : (g + 1) * modes_dev, :]
    mixer[...] = mixer_f32[...].astype(jnp.bfloat16)

    def as_column(row):
        return jnp.broadcast_to(row.astype(jnp.float32), (LANES, LANES)).T.astype(jnp.int32)

    lanes = lax.broadcasted_iota(jnp.int32, (LANES, LANES), 1)
    interface_rows = send_ref.shape[1]

    def fill_pack_map():
        for side in range(2):
            shifted = lanes - lax.rem(me, per_half) * cap - side * half_lanes
            position = jnp.where((shifted >= 0) & (shifted < cap), shifted, -slot_total - 1)
            for at in range(0, interface_rows, LANES):
                slots = as_column(send_ref[:, at : at + LANES])
                low = side * interface_rows + at
                for o in range(n_space):
                    hit = position + o * cap == slots
                    pack_map[low : low + LANES, o * LANES : (o + 1) * LANES] = jnp.where(hit, 1.0, 0.0).astype(
                        jnp.bfloat16
                    )

    def fill_add_map(first, last):
        for at in range(first, last, LANES):
            rows = as_column(recv_ref[:, at : at + LANES])
            for b in range(owned_blocks):
                hit = lanes + b * LANES == rows
                add_map[at : at + LANES, b * LANES : (b + 1) * LANES] = jnp.where(hit, 1.0, 0.0).astype(
                    jnp.bfloat16
                )

    def row_weights(c):
        return stiff[:, pl.ds(c * stored, stored)].reshape(-1, block_size)

    def own_modes(column, k):
        return mixed[column, k, group]

    def half_modes(column, k):
        return mixed[column, k, pl.ds(2 * half, 2)].reshape(2 * mode_rows, block_size)

    def pair_product(c, modes):
        picked = [
            jnp.concatenate([modes(cols_ref[s, r], k) for k in range(term_count) for s in range(stored)], axis=1)
            for r in (c, c + 1)
        ]
        weights = jnp.concatenate([row_weights(c), row_weights(c + 1)], axis=1)
        product = jnp.dot(jnp.concatenate(picked, axis=0), weights, preferred_element_type=jnp.float32)
        tall = product.shape[0] // 2
        return jnp.concatenate([product[:tall, :block_size], product[tall:, block_size:]], axis=1)

    def all_modes_row(c):
        picked = [
            mixed[cols_ref[s, c], k].reshape(all_rows, block_size)
            for k in range(term_count)
            for s in range(stored)
        ]
        return jnp.dot(jnp.concatenate(picked, axis=1), row_weights(c), preferred_element_type=jnp.float32)

    def swap_copy(apply, target):
        return pltpu.make_async_remote_copy(
            src_ref=outbox.at[apply, target],
            dst_ref=inbox.at[apply, me],
            send_sem=swap_send.at[apply, target],
            recv_sem=swap_recv.at[apply, me],
            device_id={"space": target},
            device_id_type=MESH,
        )

    def arrival(apply, source):
        return pltpu.make_async_remote_copy(
            src_ref=outbox.at[apply, source],
            dst_ref=inbox.at[apply, source],
            send_sem=swap_send.at[apply, source],
            recv_sem=swap_recv.at[apply, source],
            device_id={"space": source},
            device_id_type=MESH,
        )

    def send_interface(apply):
        modes = half_modes if apply == 0 else own_modes
        interface = jnp.concatenate(
            [pair_product(c, modes).astype(jnp.bfloat16) for c in range(owned_blocks, out_blocks, 2)], axis=1
        )
        if apply == 0:
            interface = jnp.concatenate([interface[:mode_rows], interface[mode_rows:]], axis=1)
        packed = jnp.dot(
            interface, pack_map[0 : interface.shape[1], :], preferred_element_type=jnp.float32
        ).astype(jnp.bfloat16)
        for o in range(n_space):
            outbox[apply, o] = packed[:, o * LANES : (o + 1) * LANES]
        for other in others:
            swap_copy(apply, other).start()
        inbox[apply, me] = outbox[apply, me]

    def take_interface(apply):
        for other in others:
            arrival(apply, other).wait_recv()
        pieces = []
        for first in range(0, n_space, per_half):
            piece = inbox[apply, first].astype(jnp.float32)
            for source in range(first + 1, first + per_half):
                piece = piece + inbox[apply, source].astype(jnp.float32)
            pieces.append(piece)
        left = lax.broadcasted_iota(jnp.int32, (mode_rows, LANES), 1) < half_lanes
        low, high = [], []
        for even, odd in zip(pieces[0::2], pieces[1::2]):
            low.append(jnp.where(left, even, pltpu.roll(odd, half_lanes, 1)))
            high.append(jnp.where(left, pltpu.roll(even, half_lanes, 1), odd))
        low = jnp.concatenate(low, axis=1).astype(jnp.bfloat16)
        if apply == 1:
            return low
        return jnp.concatenate([low, jnp.concatenate(high, axis=1).astype(jnp.bfloat16)], axis=0)

    def mix_groups(c, groups):
        whole = field[c].reshape(all_rows, chunk_dofs)
        product = jnp.dot(
            mixer[:, groups].reshape(-1, LANES), whole, preferred_element_type=jnp.float32
        ).astype(jnp.bfloat16)
        product = product.reshape(term_count, -1, mode_rows, chunk_dofs)
        for b in range(chunk_blocks):
            mixed[c * chunk_blocks + b, :, groups] = product[..., b * block_size : (b + 1) * block_size]

    def take_field(c):
        field_hop(0, c).wait_recv()
        field_hop(2, c).wait_recv()

    for c in range(chunk_count):
        field_hop(1, c).wait_recv()
        field_hop(2, c).start()
        if c == 0:
            fill_pack_map()
        elif c < chunk_count - 1:
            middle = slot_total // 2
            fill_add_map(*((0, middle) if c == 1 else (middle, slot_total)))
        if c > 0:
            take_field(c - 1)
            mix_groups(c - 1, slice(None))
    take_field(chunk_count - 1)
    mix_groups(chunk_count - 1, pl.ds(2 * half, 2))
    loads[0].wait()
    send_interface(0)
    mix_groups(chunk_count - 1, pl.ds(2 - 2 * half, 2))
    loads[1].wait()
    for p in range(half_blocks):
        sums[half, p] = all_modes_row(half * half_blocks + p).astype(jnp.bfloat16)
        sums_hop(p).start()
    own_mixer = mixer[:, group].reshape(term_count * mode_rows, LANES)
    for p in range(half_blocks):
        sums_hop(p).wait_recv()
    for c in range(chunk_count):
        blocks_now = range(c * chunk_blocks, (c + 1) * chunk_blocks)
        own = jnp.concatenate([sums[b // half_blocks, b % half_blocks] for b in blocks_now], axis=1)
        own_mixed[c] = jnp.dot(own_mixer, own, preferred_element_type=jnp.float32)
    arrived[half] = take_interface(0).reshape(2, mode_rows, slot_total)
    arrived_hop().start()
    arrived_hop().wait_recv()

    arrived_all = arrived[...].reshape(all_rows, slot_total)
    arrived_mixed = jnp.dot(own_mixer, arrived_all, preferred_element_type=jnp.float32).astype(jnp.bfloat16)
    for c in range(chunk_count):
        span = slice(c * chunk_dofs, (c + 1) * chunk_dofs)
        added = jnp.dot(arrived_mixed, add_map[:, span], preferred_element_type=jnp.float32)
        product = (own_mixed[c] + added).astype(jnp.bfloat16)
        product = product.reshape(term_count, mode_rows, chunk_dofs)
        for b in range(chunk_blocks):
            mixed[c * chunk_blocks + b, :, group] = product[:, :, b * block_size : (b + 1) * block_size]

    send_interface(1)
    own_at = pl.ds(pl.multiple_of(group * mode_rows, mode_rows), mode_rows)
    own_arrived = arrived[group // 2, half]
    for c in range(chunk_count):
        span = slice(c * chunk_dofs, (c + 1) * chunk_dofs)
        added = jnp.dot(own_arrived, add_map[:, span], preferred_element_type=jnp.float32)
        blocks_now = range(c * chunk_blocks, (c + 1) * chunk_blocks)
        own = jnp.concatenate([sums[b // half_blocks, b % half_blocks, own_at, :] for b in blocks_now], axis=1)
        out_ref[0, :, span] = (own.astype(jnp.float32) + added)[0:modes_dev, :].astype(jnp.bfloat16)
    for load in loads[2:]:
        load.wait()
    rows_now = [pair_product(c, own_modes) for c in range(0, owned_blocks, 2)]
    last_arrived = take_interface(1)
    for c in range(chunk_count):
        span = slice(c * chunk_dofs, (c + 1) * chunk_dofs)
        added = jnp.dot(last_arrived, add_map[:, span], preferred_element_type=jnp.float32)
        own = jnp.concatenate(rows_now[c * chunk_blocks // 2 : (c + 1) * chunk_blocks // 2], axis=1)
        out_ref[1, :, span] = (own + added)[0:modes_dev, :].astype(jnp.bfloat16)

    for kind in range(3):
        for c in range(chunk_count):
            field_hop(kind, c).wait_send()
    for p in range(half_blocks):
        sums_hop(p).wait_send()
    arrived_hop().wait_send()
    for apply in range(2):
        for other in others:
            swap_copy(apply, other).wait_send()


def local(n_space, modes_in, blocks, block_cols, send_slot, recv_row, mix_cols, mix_coef):
    modes_dev, owned_dofs = modes_in.shape
    term_count, block_total, block_size, _ = blocks.shape
    mode_rows = -(-modes_dev // 16) * 16
    chunk_count = MODE_GROUPS
    chunk_dofs = owned_dofs // chunk_count
    owned_blocks = owned_dofs // block_size
    slot_total = recv_row.shape[0]
    interface_rows = send_slot.shape[0]
    vmem = pl.BlockSpec(memory_space=pltpu.VMEM)
    out = jax.ShapeDtypeStruct((2, modes_dev, owned_dofs), jnp.bfloat16)
    call = pl.pallas_call(
        functools.partial(kernel, n_space),
        out_shape=out,
        in_specs=[
            vmem,
            pl.BlockSpec(memory_space=pltpu.HBM),
            pl.BlockSpec(memory_space=pltpu.SMEM),
            vmem,
            vmem,
            vmem,
            vmem,
        ],
        out_specs=vmem,
        scratch_shapes=[
            pltpu.VMEM(blocks.shape, jnp.bfloat16),
            pltpu.VMEM((chunk_count, MODE_GROUPS, mode_rows, chunk_dofs), jnp.bfloat16),
            pltpu.VMEM((2, owned_blocks // 2, MODE_GROUPS * mode_rows, block_size), jnp.bfloat16),
            pltpu.VMEM((2, 2, mode_rows, slot_total), jnp.bfloat16),
            pltpu.VMEM((owned_blocks, term_count, MODE_GROUPS, mode_rows, block_size), jnp.bfloat16),
            pltpu.VMEM((term_count, LANES, LANES), jnp.float32),
            pltpu.VMEM((term_count, MODE_GROUPS, mode_rows, LANES), jnp.float32),
            pltpu.VMEM((term_count, MODE_GROUPS, mode_rows, LANES), jnp.bfloat16),
            pltpu.VMEM((2 * interface_rows, n_space * LANES), jnp.bfloat16),
            pltpu.VMEM((slot_total, owned_dofs), jnp.bfloat16),
            pltpu.VMEM((chunk_count, term_count * mode_rows, chunk_dofs), jnp.float32),
            pltpu.VMEM((2, n_space, mode_rows, LANES), jnp.bfloat16),
            pltpu.VMEM((2, n_space, mode_rows, LANES), jnp.bfloat16),
            pltpu.SemaphoreType.DMA((3,)),
            pltpu.SemaphoreType.DMA((3, chunk_count + owned_blocks // 2 + 1)),
            pltpu.SemaphoreType.DMA((3, chunk_count + owned_blocks // 2 + 1)),
            pltpu.SemaphoreType.DMA((2, n_space)),
            pltpu.SemaphoreType.DMA((2, n_space)),
        ],
        compiler_params=pltpu.CompilerParams(
            collective_id=0, has_side_effects=True, vmem_limit_bytes=56 * 1024 * 1024
        ),
    )
    results = call(
        modes_in,
        blocks,
        block_cols.T,
        send_slot.reshape(1, -1),
        recv_row.reshape(1, -1),
        mix_cols.transpose(0, 2, 1),
        mix_coef.transpose(0, 2, 1),
    )

    return results[0], results[1]


def solution(mesh):
    in_specs = (
        P("mode", "space"),
        P(None, "space", None, None),
        P("space", None),
        P("space"),
        P("space"),
        P(),
        P(),
    )
    out_specs = (P("mode", "space"), P("mode", "space"))
    body = functools.partial(local, mesh.shape["space"])
    return jax.shard_map(body, mesh=mesh, in_specs=in_specs, out_specs=out_specs, check_vma=False)
```
